32 devices in a mesh: row: 8 (over y, x, core), col: 4 (over z).
Axes of the slice: x: 2, y: 2, z: 4, core: 2. Of those that a mesh axis runs over, the one named last changes fastest.
Arguments:
- momentum: float32 [8192, 16384], P('row', 'col'), may hold values from -6 to 6
- right_factor: float32 [16384, 256], P('col'), may hold values from -0.046875 to 0.046875
Outputs:
- new_momentum: float32 [8192, 16384], P('row', 'col')
- update: float32 [8192, 16384], P('row', 'col')
The draws below stay inside these ranges and needn't reach their ends.
All inputs are finite; a program needn't handle non-finite values.
Results may differ from the reference program's by a relative error of at most 0.0001.
Values sent between devices are 32-bit elements; how exact they have to be, the bound alone decides.
No kernel may reach another device: no remote copies, remote signals or barrier semaphores. Data moves between devices by JAX's collectives and lax.ppermute only.
A program may use at most 128 MiB of HBM per device.

```python
import math
import jax
import jax.numpy as jnp
from jax import lax

ROWS = 8192
COLS = 16384
RANK = 256
PASSES = 1


def block_levels(stream_key, dims, cuts, least, largest):
    loudness, own = 1.0, jax.random.fold_in(stream_key, 6)
    for axis_at, blocks in cuts:
        draws = jnp.exp(jax.random.uniform(jax.random.fold_in(own, axis_at), (blocks,), jnp.float32, least / len(cuts), largest / len(cuts)))
        loudness = loudness * jnp.repeat(draws, dims[axis_at] // blocks).reshape([-1 if axis == axis_at else 1 for axis in range(len(dims))])
    return loudness


def bell_draw(stream_key, shape, spread, reach, pieces=(), held_as=jnp.bfloat16):
    level = block_levels(stream_key, shape, pieces, -0.22, 0.18) if pieces else 1.0
    values = jax.random.normal(stream_key, shape, jnp.float32) * spread * level
    return jnp.minimum(jnp.maximum(values, -reach), reach).astype(held_as)


def setup_inputs(seed: int = 0) -> dict:
    streams_of = jax.random.split(jax.random.key(seed), 3)
    momentum = bell_draw(streams_of[0], (ROWS, COLS), 1.0, 6.0, ((0, 8), (1, 4)), jnp.float32)
    right_factor = bell_draw(streams_of[1], (COLS, RANK), COLS ** -0.5, 0.046875, ((0, 4),), jnp.float32)
    return {"momentum": momentum, "right_factor": right_factor}


def orthonormal(left_rows, gram_sum):
    lower_tri = jnp.linalg.cholesky(gram_sum)
    return jax.scipy.linalg.solve_triangular(lower_tri, left_rows.T, lower=True).T

def reference(momentum, right_factor):
    highest = lax.Precision.HIGHEST
    factor_q = right_factor
    left_orth = None
    right_full = None
    for turn in range(PASSES):
        left_rows = jnp.dot(momentum, factor_q, precision=highest)
        gram_sum = jnp.dot(left_rows.T, left_rows, precision=highest)
        left_orth = orthonormal(left_rows, gram_sum)
        right_full = jnp.dot(momentum.T, left_orth, precision=highest)
        squares = lax.optimization_barrier(jnp.sum(right_full * right_full, axis=0))
        factor_q = right_full / jnp.sqrt(squares + 1e-06)
    new_momentum = momentum - 0.5 * jnp.dot(left_orth, right_full.T, precision=highest)
    scale = math.sqrt(ROWS * COLS / RANK)
    update = scale * jnp.dot(left_orth, factor_q.T, precision=highest)
    return (new_momentum, update)
```

```python
import math

import jax
import jax.numpy as jnp
from jax import lax
from jax.experimental import pallas as pl
from jax.experimental.pallas import tpu as pltpu
from jax.sharding import PartitionSpec as P

F32 = jnp.float32
BF16 = jnp.bfloat16
HIGHEST = lax.Precision.HIGHEST
VMEM_LIMIT = 48 * 1024 * 1024
LINE = 4
RING = 8


def split(x):
    high = x.astype(BF16)
    return high, (x - high.astype(F32)).astype(BF16)


def dot(a, b):
    return jnp.dot(a, b, preferred_element_type=F32)


def params(*semantics):
    return pltpu.CompilerParams(vmem_limit_bytes=VMEM_LIMIT, dimension_semantics=semantics)


def cost(flops, bytes_accessed):
    return pl.CostEstimate(flops=int(flops), bytes_accessed=int(bytes_accessed), transcendentals=0)


def left_kernel(m_ref, q_ref, out_ref):
    m_high, m_low = split(m_ref[...])
    q_high, q_low = split(q_ref[...])
    part = dot(m_high, q_high) + dot(m_high, q_low) + dot(m_low, q_high)

    @pl.when(pl.program_id(0) == 0)
    def _():
        out_ref[...] = part

    @pl.when(pl.program_id(0) > 0)
    def _():
        out_ref[...] += part


def left_piece(momentum, factor, piece, rows):
    cols, rank = factor.shape
    tile = 1024
    return pl.pallas_call(
        left_kernel,
        grid=(cols // tile,),
        in_specs=[
            pl.BlockSpec((rows, tile), lambda k: (piece, k)),
            pl.BlockSpec((tile, rank), lambda k: (k, 0)),
        ],
        out_specs=pl.BlockSpec((rows, rank), lambda k: (0, 0)),
        out_shape=jax.ShapeDtypeStruct((rows, rank), F32),
        compiler_params=params("arbitrary"),
        cost_estimate=cost(6 * rows * cols * rank, 4 * cols * (rows + rank)),
        name="left",
    )(momentum, factor)


def raw_kernel(pieces, order_ref, *refs):
    left_refs = refs[:pieces]
    m_ref, out_ref, high_ref, low_ref = refs[pieces:]

    @pl.when(pl.program_id(0) == 0)
    def _():
        at = 0
        for ref in left_refs:
            rows = ref.shape[0]
            high, low = split(ref[...].T)
            high_ref[:, at : at + rows] = high
            low_ref[:, at : at + rows] = low
            at += rows

    m_high, m_low = split(m_ref[...])
    high = high_ref[...]
    out_ref[0] = dot(high, m_high) + dot(high, m_low) + dot(low_ref[...], m_high)


def raw_chunks(order, lefts, momentum, width):
    rows, cols = momentum.shape
    rank = lefts[0].shape[1]
    count = order.shape[0]
    whole = [pl.BlockSpec(x.shape, lambda s, order: (0, 0)) for x in lefts]
    return pl.pallas_call(
        lambda *refs: raw_kernel(len(lefts), *refs),
        grid_spec=pltpu.PrefetchScalarGridSpec(
            num_scalar_prefetch=1,
            grid=(count,),
            in_specs=whole + [pl.BlockSpec((rows, width), lambda s, order: (0, order[s]))],
            out_specs=pl.BlockSpec((1, rank, width), lambda s, order: (s, 0, 0)),
            scratch_shapes=[pltpu.VMEM((rank, rows), BF16), pltpu.VMEM((rank, rows), BF16)],
        ),
        out_shape=jax.ShapeDtypeStruct((count, rank, width), F32),
        compiler_params=params("arbitrary"),
        cost_estimate=cost(6 * rows * rank * width * count, 4 * count * width * (rows + rank)),
        name="raw_right",
    )(order, *lefts, momentum)


def gram_kernel(pieces, core_ref, *refs):
    out_ref = refs[pieces]
    total = None
    for ref in refs[:pieces]:
        part = lax.dot_general(
            ref[...], ref[...], (((0,), (0,)), ((), ())), precision=HIGHEST, preferred_element_type=F32
        )
        total = part if total is None else total + part
    half = total.shape[0] // 2
    first = core_ref[0] == 0
    out_ref[0] = jnp.where(first, total[:half], total[half:])
    out_ref[1] = jnp.where(first, total[half:], total[:half])


def gram_halves(core, lefts):
    rank = lefts[0].shape[1]
    smem = pl.BlockSpec(memory_space=pltpu.SMEM)
    vmem = pl.BlockSpec(memory_space=pltpu.VMEM)
    return pl.pallas_call(
        lambda *refs: gram_kernel(len(lefts), *refs),
        in_specs=[smem] + [vmem] * len(lefts),
        out_specs=vmem,
        out_shape=jax.ShapeDtypeStruct((2, rank // 2, rank), F32),
        compiler_params=params(),
        cost_estimate=cost(12 * rank * rank * 1024, 2**21),
        name="gram",
    )(core, *lefts)


def inverse_factor(work_ref, rank, block):
    lanes = 128
    lane_at = lax.broadcasted_iota(jnp.int32, (block, lanes), 1)
    row_at = lax.broadcasted_iota(jnp.int32, (block, lanes), 0)
    for start in range(0, rank, block):
        tile, offset = start // lanes * lanes, start % lanes
        stop = start + block
        diag = work_ref[start:stop, tile : tile + lanes]
        eye = jnp.where(lane_at == row_at, 1.0, 0.0).astype(F32)
        for j in range(block):
            pivot = diag[j : j + 1, offset + j : offset + j + 1]
            ratio = diag[:, offset + j : offset + j + 1] * (1.0 / pivot)
            ratio = jnp.where(row_at[:, :1] > j, ratio, 0.0)
            if j + 1 < block:
                new_eye = eye - ratio * eye[j : j + 1, :]
                diag = diag - ratio * diag[j : j + 1, :]
                eye = new_eye
        pivots = jnp.sum(jnp.where(lane_at == row_at + offset, diag, 0.0), axis=1, keepdims=True)
        small = (eye / jnp.sqrt(pivots))[:, :block]
        end = min(2 * rank, -(-(rank + stop) // lanes) * lanes)
        done = jnp.dot(small, work_ref[start:stop, tile:end], precision=HIGHEST, preferred_element_type=F32)
        work_ref[start:stop, tile:end] = done
        if stop < rank:
            below = done[:, stop - tile : rank - tile]
            work_ref[stop:rank, tile:end] -= lax.dot_general(
                below, done, (((0,), (0,)), ((), ())), precision=HIGHEST, preferred_element_type=F32
            )


def factor_kernel(pieces, core_ref, kept_ref, sent_ref, *refs):
    left_refs = refs[:pieces]
    inv_ref, orth_ref, work_ref = refs[pieces:]
    half, rank = kept_ref.shape
    first = core_ref[0] == 0
    work_ref[:half, :rank] = jnp.where(first, kept_ref[...], sent_ref[...])
    work_ref[half:, :rank] = jnp.where(first, sent_ref[...], kept_ref[...])
    rows = lax.broadcasted_iota(jnp.int32, (rank, rank), 0)
    cols = lax.broadcasted_iota(jnp.int32, (rank, rank), 1)
    work_ref[:, rank:] = jnp.where(rows == cols, 1.0, 0.0).astype(F32)
    inverse_factor(work_ref, rank, 32)
    inverse = jnp.where(rows >= cols, work_ref[:, rank:], 0.0)
    inv_ref[...] = inverse
    at = 0
    for ref in left_refs:
        size = ref.shape[0]
        orth_ref[at : at + size, :] = lax.dot_general(
            ref[...], inverse, (((1,), (1,)), ((), ())), precision=HIGHEST, preferred_element_type=F32
        )
        at += size


def factor(core, kept, sent, lefts):
    rank = kept.shape[1]
    rows = sum(x.shape[0] for x in lefts)
    smem = pl.BlockSpec(memory_space=pltpu.SMEM)
    vmem = pl.BlockSpec(memory_space=pltpu.VMEM)
    return pl.pallas_call(
        lambda *refs: factor_kernel(len(lefts), *refs),
        in_specs=[smem] + [vmem] * (2 + len(lefts)),
        out_specs=[vmem, vmem],
        out_shape=[jax.ShapeDtypeStruct((rank, rank), F32), jax.ShapeDtypeStruct((rows, rank), F32)],
        scratch_shapes=[pltpu.VMEM((rank, 2 * rank), F32)],
        compiler_params=params(),
        cost_estimate=cost(2 * 10**10, 2**22),
        name="factor",
    )(core, kept, sent, *lefts)


def square_kernel(inv_ref, raw_ref, out_ref):
    right = jnp.dot(inv_ref[...], raw_ref[0], precision=HIGHEST, preferred_element_type=F32)
    ones = jnp.ones((8, right.shape[1]), F32)
    out_ref[...] = lax.dot_general(
        ones, right * right, (((1,), (1,)), ((), ())), precision=HIGHEST, preferred_element_type=F32
    )


def square_row(inverse, raw):
    rank = inverse.shape[0]
    return pl.pallas_call(
        square_kernel,
        out_shape=jax.ShapeDtypeStruct((8, rank), F32),
        compiler_params=params(),
        cost_estimate=cost(12 * rank * rank * raw.shape[2], 2**20),
        name="squares",
    )(inverse, raw)


def operand_kernel(count, scale, *refs):
    square_refs = refs[:count]
    orth_ref, high_ref, low_ref = refs[count:]
    squares = square_refs[0][...]
    for ref in square_refs[1:]:
        squares = squares + ref[...]
    norm = scale / jnp.sqrt(squares[:1] + 1e-06)
    orth = orth_ref[...]
    high_ref[0], low_ref[0] = split(orth * -0.5)
    high_ref[1], low_ref[1] = split(orth * norm)


def operands(squares, orth, scale):
    rows, rank = orth.shape
    shape = jax.ShapeDtypeStruct((2, rows, rank), BF16)
    return pl.pallas_call(
        lambda *refs: operand_kernel(len(squares), scale, *refs),
        out_shape=[shape, shape],
        compiler_params=params(),
        cost_estimate=cost(rows * rank * 10, rows * rank * 12),
        name="operands",
    )(*squares, orth)


def output_kernel(chained, order_ref, high_ref, low_ref, inv_ref, raw_ref, m_ref, *refs):
    new_ref, update_ref, right_high_ref, right_low_ref = refs[2 if chained else 0 :]

    @pl.when(pl.program_id(0) == 0)
    def _():
        inv_high, inv_low = split(inv_ref[...])
        raw_high, raw_low = split(raw_ref[0])
        right = dot(inv_high, raw_high) + dot(inv_high, raw_low) + dot(inv_low, raw_high)
        right_high_ref[...], right_low_ref[...] = split(right)

    right_high, right_low = right_high_ref[...], right_low_ref[...]
    new_ref[...] = m_ref[...] + (
        dot(high_ref[0], right_high) + dot(high_ref[0], right_low) + dot(low_ref[0], right_high)
    )
    update_ref[...] = dot(high_ref[1], right_high) + dot(high_ref[1], right_low) + dot(low_ref[1], right_high)


def output_chunk(order, high, low, inverse, raw, momentum, before):
    rows, cols = momentum.shape
    _, rank, width = raw.shape
    tile = 256
    operand = pl.BlockSpec((2, tile, rank), lambda i, order: (0, i, 0))
    block = pl.BlockSpec((tile, width), lambda i, order: (i, order[0]))
    whole = jax.ShapeDtypeStruct((rows, cols), F32)
    return pl.pallas_call(
        lambda *refs: output_kernel(bool(before), *refs),
        grid_spec=pltpu.PrefetchScalarGridSpec(
            num_scalar_prefetch=1,
            grid=(rows // tile,),
            in_specs=[
                operand,
                operand,
                pl.BlockSpec((rank, rank), lambda i, order: (0, 0)),
                pl.BlockSpec((1, rank, width), lambda i, order: (0, 0, 0)),
                block,
            ]
            + [pl.BlockSpec(memory_space=pl.ANY)] * len(before),
            out_specs=[block, block],
            scratch_shapes=[pltpu.VMEM((rank, width), BF16), pltpu.VMEM((rank, width), BF16)],
        ),
        out_shape=[whole, whole],
        input_output_aliases={6: 0, 7: 1} if before else {},
        compiler_params=params("arbitrary"),
        cost_estimate=cost(12 * rows * rank * width, 12 * rows * width),
        name="outputs",
    )(order, high, low, inverse, raw, momentum, *before)


def line_sum(part, inner):
    held = part + lax.ppermute(part, "col", [(0, 1), (3, 2)])
    held = held + lax.ppermute(held, "col", [(1, 2), (2, 1)])
    return jnp.where(inner, held, lax.ppermute(held, "col", [(1, 0), (2, 3)]))


PAIR = [(r, r ^ 1) for r in range(RING)]
NEAR = [(r, r ^ (2 if r % 2 == 0 else 4)) for r in range(RING)]
FAR = [(r, r ^ (4 if r % 2 == 0 else 2)) for r in range(RING)]


def local(momentum, right_factor, scale):
    rows, cols = momentum.shape
    me, at = lax.axis_index("row"), lax.axis_index("col")
    core = me % 2
    first, second = me // 2 % 2, me // 4
    low_id = jnp.where(core == 0, 2 * first + second, 2 * second + first)
    pair_id = jnp.where(core == 0, 2 * second + first, 2 * first + second)
    slots = jnp.arange(4, dtype=jnp.int32)
    mine = (4 * core + (slots ^ low_id)).astype(jnp.int32)
    theirs = (4 * (1 - core) + (slots ^ pair_id)).astype(jnp.int32)
    core = core.astype(jnp.int32).reshape(1)
    width = cols // RING
    inner = (at > 0) & (at < LINE - 1)

    pieces = 4
    lefts = [left_piece(momentum, right_factor, piece, rows // pieces) for piece in range(pieces)]
    lefts = [line_sum(part, inner) for part in lefts]

    def raw(order, a, b):
        return raw_chunks(jnp.stack([order[a], order[b]]), lefts, momentum, width)

    sent_far, kept_far = raw(theirs, 3, 2), raw(mine, 3, 2)
    sent_near, kept_near = raw(theirs, 1, 0), raw(mine, 1, 0)
    got = lax.ppermute(sent_far, "row", PAIR)
    slot_3, slot_2 = kept_far[:1] + got[:1], kept_far[1:] + got[1:]
    got_1 = lax.ppermute(slot_3, "row", NEAR)
    got_0 = lax.ppermute(slot_2, "row", NEAR)
    got = lax.ppermute(sent_near, "row", PAIR)
    slot_1 = kept_near[:1] + got[:1] + got_1
    got_own = lax.ppermute(slot_1, "row", FAR)
    own = kept_near[1:] + got[1:] + got_0 + got_own

    halves = gram_halves(core, lefts)
    kept = halves[0] + lax.ppermute(halves[1], "row", PAIR)
    kept = kept + lax.ppermute(kept, "row", NEAR)
    kept = kept + lax.ppermute(kept, "row", FAR)
    inverse, orth = factor(core, kept, lax.ppermute(kept, "row", PAIR), lefts)

    chunk_1 = lax.ppermute(own, "row", FAR)
    chunk_2 = lax.ppermute(own, "row", NEAR)
    chunk_3 = lax.ppermute(chunk_1, "row", NEAR)
    chunks = [own, chunk_1, chunk_2, chunk_3]
    others = [lax.ppermute(chunk, "row", PAIR) for chunk in chunks]

    squares = square_row(inverse, own)
    for step in (1, 2, 4):
        squares = squares + lax.ppermute(squares, "row", [(r, r ^ step) for r in range(RING)])
    squares = [squares] + [lax.ppermute(squares, "col", [(c, c ^ d) for c in range(LINE)]) for d in (1, 2, 3)]
    high, low = operands(squares, orth, scale)

    outs = []
    for slot in range(4):
        for order, raws in ((mine, chunks), (theirs, others)):
            outs = output_chunk(order[slot : slot + 1], high, low, inverse, raws[slot], momentum, outs)
    return tuple(outs)


def general(momentum, right_factor, scale):
    left = lax.psum(jnp.dot(momentum, right_factor, precision=HIGHEST), "col")
    gram_part = jnp.dot(left.T, left, precision=HIGHEST)
    raw_part = jnp.dot(left.T, momentum, precision=HIGHEST)
    gram, raw = lax.psum((gram_part, raw_part), "row")
    lower = jnp.linalg.cholesky(gram)
    orth = jax.scipy.linalg.solve_triangular(lower, left.T, lower=True).T
    right = jax.scipy.linalg.solve_triangular(lower, raw, lower=True)
    squares = lax.psum(jnp.sum(right * right, axis=1, keepdims=True), "col")
    factor_q = right / jnp.sqrt(squares + 1e-06)
    new = momentum - 0.5 * jnp.dot(orth, right, precision=HIGHEST)
    return new, scale * jnp.dot(orth, factor_q, precision=HIGHEST)


def solution(mesh):
    by_hand = mesh.shape["row"] == RING and mesh.shape["col"] == LINE
    program = local if by_hand else general

    def run(momentum, right_factor):
        rows, cols = momentum.shape
        scale = math.sqrt(rows * cols / right_factor.shape[1])
        return jax.shard_map(
            lambda m, q: program(m, q, scale),
            mesh=mesh,
            in_specs=(P("row", "col"), P("col", None)),
            out_specs=(P("row", "col"), P("row", "col")),
            check_vma=False,
        )(momentum, right_factor)

    return run
```

```python
import math

import jax
import jax.numpy as jnp
from jax import lax
from jax.experimental import pallas as pl
from jax.experimental.pallas import tpu as pltpu
from jax.sharding import PartitionSpec as P

F32 = jnp.float32
BF16 = jnp.bfloat16
HIGHEST = lax.Precision.HIGHEST
VMEM_LIMIT = 20 * 1024 * 1024
SMEM = pl.BlockSpec(memory_space=pltpu.SMEM)
VMEM = pl.BlockSpec(memory_space=pltpu.VMEM)
HBM = pl.BlockSpec(memory_space=pltpu.HBM)
ANY = pl.BlockSpec(memory_space=pl.ANY)
LINE = 4
RING = 8


def split(x):
    high = x.astype(BF16)
    return high, (x - high.astype(F32)).astype(BF16)


def dot(a, b):
    return jnp.dot(a, b, preferred_element_type=F32)


def params():
    return pltpu.CompilerParams(vmem_limit_bytes=VMEM_LIMIT)


def cost(flops, bytes_accessed):
    return pl.CostEstimate(flops=int(flops), bytes_accessed=int(bytes_accessed), transcendentals=0)


def in_vmem(x):
    return pltpu.with_memory_space_constraint(x, pltpu.VMEM)


def in_hbm(x):
    return pltpu.with_memory_space_constraint(x, pltpu.HBM)


def three(high, low, axis):
    return jnp.concatenate([high, high, low], axis=axis)


def three_other(high, low, axis):
    return jnp.concatenate([high, low, high], axis=axis)


def fetch_kernel(m_hbm, q_hbm, m_ref, high_ref, low_ref, q_ref, m_sem, q_sem):
    half = q_ref.shape[0] // 2
    spans = [pl.ds(k * half, half) for k in range(2)]
    copies = [pltpu.make_async_copy(q_hbm.at[span], q_ref.at[span], q_sem.at[k]) for k, span in enumerate(spans)]
    whole = pltpu.make_async_copy(m_hbm, m_ref, m_sem)
    for copy in copies:
        copy.start()
    whole.start()
    for copy, span in zip(copies, spans):
        copy.wait()
        high_ref[span, :], low_ref[span, :] = split(q_ref[span, :])
    whole.wait()


def fetch(momentum, factor):
    cols, rank = factor.shape
    return pl.pallas_call(
        fetch_kernel,
        in_specs=[HBM, HBM],
        out_specs=[ANY, VMEM, VMEM],
        out_shape=[
            pltpu.VMEM(momentum.shape, F32),
            pltpu.VMEM((cols, rank), BF16),
            pltpu.VMEM((cols, rank), BF16),
        ],
        scratch_shapes=[pltpu.VMEM((cols, rank), F32), pltpu.SemaphoreType.DMA, pltpu.SemaphoreType.DMA((2,))],
        compiler_params=params(),
        cost_estimate=cost(cols * rank, 4 * cols * (momentum.shape[0] + rank)),
        name="fetch",
    )(in_hbm(momentum), in_hbm(factor))


def left_kernel(at, m_ref, high_ref, low_ref, out_ref):
    half = high_ref.shape[0] // 2
    total = None
    for k in range(2):
        span = pl.ds(k * half, half)
        piece = m_ref[pl.ds(at, out_ref.shape[0]), span]
        part = dot(three(*split(piece), 1), three_other(high_ref[span, :], low_ref[span, :], 0))
        total = part if total is None else total + part
    out_ref[...] = total


def left_piece(momentum, high, low, at, size):
    cols, rank = high.shape
    return pl.pallas_call(
        lambda *refs: left_kernel(at, *refs),
        in_specs=[VMEM] * 3,
        out_specs=VMEM,
        out_shape=jax.ShapeDtypeStruct((size, rank), F32),
        compiler_params=params(),
        cost_estimate=cost(6 * size * cols * rank, 2**20),
        name="left",
    )(in_vmem(momentum), in_vmem(high), in_vmem(low))


def raw_kernel(at, groups, added, with_gram, order_ref, left_ref, m_ref, *refs):
    count = len(groups) + with_gram
    before_refs, out_refs = refs[: count * added], refs[count * added :]
    left = left_ref[...]
    lhs = three(*split(left.T), 1)
    if with_gram:
        gram = full_dot(left, left, ((0,), (0,)))
        out_refs[-1][...] = before_refs[-1][...] + gram if added else gram
    for g, places in enumerate(groups):
        width = out_refs[g].shape[2]
        for s, place in enumerate(places):
            span = pl.ds(pl.multiple_of(order_ref[place] * width, width), width)
            part = dot(lhs, three_other(*split(m_ref[pl.ds(at, left.shape[0]), span]), 0))
            out_refs[g][s] = before_refs[g][s] + part if added else part


def raw_pieces(order, groups, left, momentum, at, before, with_gram):
    rows, rank = left.shape
    width = momentum.shape[1] // order.shape[0]
    chunks = sum(len(places) for places in groups)
    shapes = [jax.ShapeDtypeStruct((len(places), rank, width), F32) for places in groups]
    shapes += [jax.ShapeDtypeStruct((rank, rank), F32)] * with_gram
    return pl.pallas_call(
        lambda *refs: raw_kernel(at, groups, bool(before), with_gram, *refs),
        in_specs=[SMEM] + [VMEM] * (2 + len(before)),
        out_specs=[VMEM] * len(shapes),
        out_shape=shapes,
        compiler_params=params(),
        cost_estimate=cost(6 * rows * rank * width * chunks, 2**20),
        name="raw_right",
    )(order, left, in_vmem(momentum), *before)


def gram_kernel(chunks, order_ref, left_ref, before_ref, out_ref):
    left = left_ref[...]
    total = before_ref[...] + full_dot(left, left, ((0,), (0,)))
    half = total.shape[0] // 2
    first = order_ref[0] < chunks
    out_ref[0] = jnp.where(first, total[:half], total[half:])
    out_ref[1] = jnp.where(first, total[half:], total[:half])


def gram_halves(order, left, before):
    rank = left.shape[1]
    return pl.pallas_call(
        lambda *refs: gram_kernel(order.shape[0] // 2, *refs),
        in_specs=[SMEM, VMEM, VMEM],
        out_specs=VMEM,
        out_shape=jax.ShapeDtypeStruct((2, rank // 2, rank), F32),
        compiler_params=params(),
        cost_estimate=cost(12 * rank * rank * left.shape[0], 2**20),
        name="gram",
    )(order, left, before)


def full_dot(a, b, contract=((1,), (0,))):
    return lax.dot_general(a, b, (contract, ((), ())), precision=HIGHEST, preferred_element_type=F32)


def rough_dot(a, b, contract=((1,), (0,))):
    return lax.dot_general(a.astype(BF16), b.astype(BF16), (contract, ((), ())), preferred_element_type=F32)


def newton(gram_ref, x_ref):
    rank = gram_ref.shape[0]
    rows = lax.broadcasted_iota(jnp.int32, (rank, rank), 0)
    cols = lax.broadcasted_iota(jnp.int32, (rank, rank), 1)
    eye = jnp.where(rows == cols, 1.0, 0.0).astype(F32)
    gram = gram_ref[...]
    x = eye * lax.rsqrt(jnp.sum(gram * eye, axis=1, keepdims=True))
    for times in (rough_dot, rough_dot, full_dot, full_dot):
        error = times(times(x, gram), x, ((1,), (1,))) - eye
        x = x - times(jnp.where(rows > cols, error, 0.5 * eye * error), x)
    x_ref[...] = x
    return jnp.sum(error * error), jnp.min(jnp.where(rows == cols, x, 1.0))


def eliminate(work_ref):
    rank = work_ref.shape[0]
    rows = lax.broadcasted_iota(jnp.int32, (rank, 2 * rank), 0)
    cols = lax.broadcasted_iota(jnp.int32, (rank, 2 * rank), 1)

    def step(j, carry):
        work = work_ref[...]
        row = work_ref[pl.ds(j, 1), :]
        pivot = jnp.sum(jnp.where(cols[:1] == j, row, 0.0), axis=1, keepdims=True)
        column = jnp.sum(jnp.where(cols == j, work, 0.0), axis=1, keepdims=True)
        ratio = jnp.where(rows[:, :1] > j, column * (1.0 / pivot), 0.0)
        work_ref[...] = work - ratio * row
        return carry

    lax.fori_loop(0, rank, step, 0)
    work = work_ref[...]
    pivots = jnp.sum(jnp.where(rows == cols, work, 0.0), axis=1, keepdims=True)
    return jnp.where(rows + rank >= cols, work / jnp.sqrt(pivots), 0.0)[:, rank:]


def factor_kernel(pieces, chunks, order_ref, kept_ref, sent_ref, *refs):
    left_refs = refs[:pieces]
    inv_ref, orth_ref, operand_ref, gram_ref, work_ref = refs[pieces:]
    half, rank = kept_ref.shape
    first = order_ref[0] < chunks
    gram_ref[:half] = jnp.where(first, kept_ref[...], sent_ref[...])
    gram_ref[half:] = jnp.where(first, sent_ref[...], kept_ref[...])
    before, least = newton(gram_ref, inv_ref)

    @pl.when(jnp.logical_not((before < 1e-6) & (least > 0.0)))
    def _():
        rows = lax.broadcasted_iota(jnp.int32, (rank, rank), 0)
        cols = lax.broadcasted_iota(jnp.int32, (rank, rank), 1)
        work_ref[:, :rank] = gram_ref[...]
        work_ref[:, rank:] = jnp.where(rows == cols, 1.0, 0.0).astype(F32)
        inv_ref[...] = eliminate(work_ref)

    inverse = three_other(*split(inv_ref[...]), 1)
    at = 0
    for ref in left_refs:
        size = ref.shape[0]
        orth = lax.dot_general(
            three(*split(ref[...]), 1), inverse, (((1,), (1,)), ((), ())), preferred_element_type=F32
        )
        orth_ref[at : at + size, :] = orth
        operand_ref[at : at + size, :] = three(*split(-0.5 * orth), 1)
        at += size


def factor(order, kept, sent, lefts):
    rank = kept.shape[1]
    rows = sum(x.shape[0] for x in lefts)
    return pl.pallas_call(
        lambda *refs: factor_kernel(len(lefts), order.shape[0] // 2, *refs),
        in_specs=[SMEM] + [VMEM] * (2 + len(lefts)),
        out_specs=[VMEM] * 3,
        out_shape=[
            jax.ShapeDtypeStruct((rank, rank), F32),
            jax.ShapeDtypeStruct((rows, rank), F32),
            jax.ShapeDtypeStruct((rows, 3 * rank), BF16),
        ],
        scratch_shapes=[pltpu.VMEM((rank, rank), F32), pltpu.VMEM((rank, 2 * rank), F32)],
        compiler_params=params(),
        cost_estimate=cost(5 * 10**9, 2**22),
        name="factor",
    )(order, kept, sent, *lefts)


def square_kernel(inv_ref, raw_ref, out_ref):
    right = jnp.dot(inv_ref[...], raw_ref[0], precision=HIGHEST, preferred_element_type=F32)
    ones = jnp.ones((8, right.shape[1]), F32)
    out_ref[...] = lax.dot_general(
        ones, right * right, (((1,), (1,)), ((), ())), precision=HIGHEST, preferred_element_type=F32
    )


def square_row(inverse, raw):
    rank = inverse.shape[0]
    return pl.pallas_call(
        square_kernel,
        out_shape=jax.ShapeDtypeStruct((8, rank), F32),
        compiler_params=params(),
        cost_estimate=cost(12 * rank * rank * raw.shape[2], 2**20),
        name="squares",
    )(inverse, raw)


def operand_kernel(count, scale, *refs):
    square_refs = refs[:count]
    orth_ref, operand_ref = refs[count:]
    squares = square_refs[0][...]
    for ref in square_refs[1:]:
        squares = squares + ref[...]
    norm = scale / jnp.sqrt(squares[:1] + 1e-06)
    operand_ref[...] = three(*split(orth_ref[...] * norm), 1)


def update_operand(squares, orth, scale):
    rows, rank = orth.shape
    return pl.pallas_call(
        lambda *refs: operand_kernel(len(squares), scale, *refs),
        out_shape=jax.ShapeDtypeStruct((rows, 3 * rank), BF16),
        compiler_params=params(),
        cost_estimate=cost(rows * rank * 10, rows * rank * 12),
        name="operand",
    )(*squares, orth)


def new_kernel(places, chained, order_ref, operand_ref, inv_ref, m_ref, *refs):
    count = len(places)
    raw_refs, refs = refs[:count], refs[count + chained :]
    out_hbm, right_refs, (out_ref, sem) = refs[0], refs[1 : 1 + count], refs[1 + count :]
    _, rows, width = out_ref.shape
    parts = sem.shape[1]
    tile = rows // parts
    inverse = three(*split(inv_ref[...]), 1)
    for raw_ref, right_ref in zip(raw_refs, right_refs):
        right = dot(inverse, three_other(*split(raw_ref[0]), 0))
        right_ref[...] = three_other(*split(right), 0)
    copies = []
    for s, right_ref in enumerate(right_refs):
        span = pl.ds(pl.multiple_of(order_ref[places[s]] * width, width), width)
        right = right_ref[...]
        for part in range(parts):
            at = pl.ds(part * tile, tile)
            out_ref[s, at] = m_ref[at, span] + dot(operand_ref[at, :], right)
            copies.append(pltpu.make_async_copy(out_ref.at[s, at], out_hbm.at[at, span], sem.at[s, part]))
            copies[-1].start()
    for copy in copies:
        copy.wait()


def new_chunks(order, places, operand, inverse, raws, momentum, before):
    rows, cols = momentum.shape
    _, rank, width = raws[0].shape
    count, parts = len(raws), 4
    outs = pl.pallas_call(
        lambda *refs: new_kernel(places, len(before), *refs),
        in_specs=[SMEM] + [VMEM] * (3 + count) + [HBM] * len(before),
        out_specs=[HBM] + [VMEM] * count,
        out_shape=[jax.ShapeDtypeStruct((rows, cols), F32)]
        + [jax.ShapeDtypeStruct((3 * rank, width), BF16)] * count,
        scratch_shapes=[pltpu.VMEM((count, rows, width), F32), pltpu.SemaphoreType.DMA((count, parts))],
        input_output_aliases={4 + count: 0} if before else {},
        compiler_params=params(),
        cost_estimate=cost(6 * count * rows * rank * width, 4 * count * rows * width),
        name="new_momentum",
    )(order, operand, inverse, in_vmem(momentum), *raws, *before)
    return [outs[0]], list(outs[1:])


def update_kernel(places, chained, order_ref, operand_ref, *refs):
    count = len(places)
    right_refs, (out_hbm, out_ref, sem) = refs[:count], refs[count + chained :]
    _, rows, width = out_ref.shape
    parts = sem.shape[1]
    tile = rows // parts
    copies = []
    for s, right_ref in enumerate(right_refs):
        span = pl.ds(pl.multiple_of(order_ref[places[s]] * width, width), width)
        right = right_ref[...]
        for part in range(parts):
            at = pl.ds(part * tile, tile)
            out_ref[s, at] = dot(operand_ref[at, :], right)
            copies.append(pltpu.make_async_copy(out_ref.at[s, at], out_hbm.at[at, span], sem.at[s, part]))
            copies[-1].start()
    for copy in copies:
        copy.wait()


def update_chunks(order, places, operand, rights, before, cols):
    rows = operand.shape[0]
    width = rights[0].shape[1]
    rank = rights[0].shape[0] // 3
    count, parts = len(rights), 4
    return [
        pl.pallas_call(
            lambda *refs: update_kernel(places, len(before), *refs),
            in_specs=[SMEM] + [VMEM] * (1 + count) + [HBM] * len(before),
            out_specs=HBM,
            out_shape=jax.ShapeDtypeStruct((rows, cols), F32),
            scratch_shapes=[pltpu.VMEM((count, rows, width), F32), pltpu.SemaphoreType.DMA((count, parts))],
            input_output_aliases={2 + count: 0} if before else {},
            compiler_params=params(),
            cost_estimate=cost(6 * count * rows * rank * width, 4 * count * rows * width),
            name="update",
        )(order, operand, *rights, *before)
    ]


PAIR = [(r, r ^ 1) for r in range(RING)]
NEAR = [(r, r ^ (2 if r % 2 == 0 else 4)) for r in range(RING)]
FAR = [(r, r ^ (4 if r % 2 == 0 else 2)) for r in range(RING)]
ACROSS = [(r, r ^ 6) for r in range(RING)]


def along(x, pairs):
    return lax.ppermute(x, "row", pairs)


def together(*values):
    return lax.optimization_barrier(values)


def local(momentum, right_factor, scale):
    rows, cols = momentum.shape
    me, at = lax.axis_index("row"), lax.axis_index("col")
    core, first, second = me % 2, me // 2 % 2, me // 4
    low_id = jnp.where(core == 0, 2 * first + second, 2 * second + first)
    pair_id = jnp.where(core == 0, 2 * second + first, 2 * first + second)
    slots = jnp.arange(RING, dtype=jnp.int32)
    order = jnp.where(slots < 4, 4 * core + (slots ^ low_id), 4 * (1 - core) + ((slots - 4) ^ pair_id))
    order = order.astype(jnp.int32)
    inner = (at > 0) & (at < LINE - 1)

    pieces = 4
    size = rows // pieces
    starts = [k * size for k in range(pieces)]
    resident, high, low = fetch(momentum, right_factor)
    arrived, crossed, lefts = [], [], []
    for k in range(pieces):
        if k == pieces - 1:
            high, arrived[0] = together(high, arrived[0])
        left = left_piece(resident, high, low, starts[k], size)
        arrived.append(left + lax.ppermute(left, "col", [(0, 1), (3, 2)]))
    for k in range(pieces):
        if k == pieces - 1:
            arrived[k], crossed[0] = together(arrived[k], crossed[0])
        crossed.append(arrived[k] + lax.ppermute(arrived[k], "col", [(1, 2), (2, 1)]))
    for held in crossed:
        lefts.append(jnp.where(inner, held, lax.ppermute(held, "col", [(1, 0), (2, 3)])))

    groups = ((7, 6), (3, 2), (5, 4), (1, 0))
    sums = []
    for k in range(pieces - 1):
        sums = raw_pieces(order, groups, lefts[k], resident, starts[k], sums, 1)

    def last(order, group):
        return raw_pieces(order, groups[group : group + 1], lefts[-1], resident, starts[-1], [sums[group]], 0)[0]

    sent_far = last(order, 0)
    order_1, sent_far = together(order, sent_far)
    halves = gram_halves(order_1, lefts[-1], sums[-1])
    order_2, halves = together(order_1, halves)
    kept_far = last(order_2, 1)
    order_3, kept_far = together(order_2, kept_far)
    sent_near, kept_near = last(order_3, 2), last(order_3, 3)

    got = along(sent_far, PAIR)
    slot_3, slot_2 = kept_far[:1] + got[:1], kept_far[1:] + got[1:]
    got_1 = along(slot_3, NEAR)
    kept = halves[0] + along(halves[1], PAIR)
    slot_2, kept = together(slot_2, kept)
    kept = kept + along(kept, NEAR) + along(kept, FAR) + along(kept, ACROSS)
    other = along(kept, PAIR)
    got_0 = along(slot_2, NEAR)
    got = along(sent_near, PAIR)
    slot_1 = kept_near[:1] + got[:1] + got_1
    got_own = along(slot_1, FAR)
    inverse, orth, operand = factor(order, kept, other, lefts)
    got_own, inverse = together(got_own, inverse)
    own = kept_near[1:] + got[1:] + got_0 + got_own

    chunk_1, chunk_2 = along(own, FAR), along(own, NEAR)
    chunks = [own, chunk_1, chunk_2, along(chunk_1, NEAR)]
    others = [along(chunk, PAIR) for chunk in chunks]

    squares = square_row(inverse, own)
    new, rights = [], []
    for slot, step in enumerate((1, 2, 4, 0)):
        if step:
            squares = squares + along(squares, [(r, r ^ step) for r in range(RING)])
        else:
            squares = [squares] + [
                lax.ppermute(squares, "col", [(c, c ^ d) for c in range(LINE)]) for d in range(1, LINE)
            ]
        raws = [chunks[slot], others[slot]]
        new, right = new_chunks(order, (slot, slot + 4), operand, inverse, raws, resident, new)
        rights += right
        if step:
            squares, new[0] = together(squares, new[0])
    operand = update_operand(squares, orth, scale)
    update = update_chunks(order, (0, 4, 1, 5), operand, rights[:4], [], cols)
    update = update_chunks(order, (2, 6, 3, 7), operand, rights[4:], update, cols)
    return new[0], update[0]


def general(momentum, right_factor, scale):
    left = lax.psum(jnp.dot(momentum, right_factor, precision=HIGHEST), "col")
    gram_part = jnp.dot(left.T, left, precision=HIGHEST)
    raw_part = jnp.dot(left.T, momentum, precision=HIGHEST)
    gram, raw = lax.psum((gram_part, raw_part), "row")
    lower = jnp.linalg.cholesky(gram)
    orth = jax.scipy.linalg.solve_triangular(lower, left.T, lower=True).T
    right = jax.scipy.linalg.solve_triangular(lower, raw, lower=True)
    squares = lax.psum(jnp.sum(right * right, axis=1, keepdims=True), "col")
    factor_q = right / jnp.sqrt(squares + 1e-06)
    new = momentum - 0.5 * jnp.dot(orth, right, precision=HIGHEST)
    return new, scale * jnp.dot(orth, factor_q, precision=HIGHEST)


def solution(mesh):
    by_hand = mesh.shape["row"] == RING and mesh.shape["col"] == LINE
    program = local if by_hand else general

    def run(momentum, right_factor):
        rows, cols = momentum.shape
        scale = math.sqrt(rows * cols / right_factor.shape[1])
        return jax.shard_map(
            lambda m, q: program(m, q, scale),
            mesh=mesh,
            in_specs=(P("row", "col"), P("col", None)),
            out_specs=(P("row", "col"), P("row", "col")),
            check_vma=False,
        )(momentum, right_factor)

    return run
```

```python
import math

import jax
import jax.numpy as jnp
from jax import lax
from jax.experimental import pallas as pl
from jax.experimental.pallas import tpu as pltpu
from jax.sharding import PartitionSpec as P

F32 = jnp.float32
BF16 = jnp.bfloat16
HIGHEST = lax.Precision.HIGHEST
VMEM_LIMIT = 20 * 1024 * 1024
SMEM = pl.BlockSpec(memory_space=pltpu.SMEM)
VMEM = pl.BlockSpec(memory_space=pltpu.VMEM)
HBM = pl.BlockSpec(memory_space=pltpu.HBM)
ANY = pl.BlockSpec(memory_space=pl.ANY)
LINE = 4
RING = 8


def split(x):
    high = x.astype(BF16)
    return high, (x - high.astype(F32)).astype(BF16)


def dot(a, b):
    return jnp.dot(a, b, preferred_element_type=F32)


def params():
    return pltpu.CompilerParams(vmem_limit_bytes=VMEM_LIMIT)


def cost(flops, bytes_accessed):
    return pl.CostEstimate(flops=int(flops), bytes_accessed=int(bytes_accessed), transcendentals=0)


def in_vmem(x):
    return pltpu.with_memory_space_constraint(x, pltpu.VMEM)


def in_hbm(x):
    return pltpu.with_memory_space_constraint(x, pltpu.HBM)


def three(high, low, axis):
    return jnp.concatenate([high, high, low], axis=axis)


def three_other(high, low, axis):
    return jnp.concatenate([high, low, high], axis=axis)


def fetch_kernel(m_hbm, q_hbm, m_ref, high_ref, low_ref, q_ref, m_sem, q_sem):
    half = q_ref.shape[0] // 2
    spans = [pl.ds(k * half, half) for k in range(2)]
    copies = [pltpu.make_async_copy(q_hbm.at[span], q_ref.at[span], q_sem.at[k]) for k, span in enumerate(spans)]
    whole = pltpu.make_async_copy(m_hbm, m_ref, m_sem)
    for copy in copies:
        copy.start()
    whole.start()
    for copy, span in zip(copies, spans):
        copy.wait()
        high_ref[span, :], low_ref[span, :] = split(q_ref[span, :])
    whole.wait()


def fetch(momentum, factor):
    cols, rank = factor.shape
    return pl.pallas_call(
        fetch_kernel,
        in_specs=[HBM, HBM],
        out_specs=[ANY, VMEM, VMEM],
        out_shape=[
            pltpu.VMEM(momentum.shape, F32),
            pltpu.VMEM((cols, rank), BF16),
            pltpu.VMEM((cols, rank), BF16),
        ],
        scratch_shapes=[pltpu.VMEM((cols, rank), F32), pltpu.SemaphoreType.DMA, pltpu.SemaphoreType.DMA((2,))],
        compiler_params=params(),
        cost_estimate=cost(cols * rank, 4 * cols * (momentum.shape[0] + rank)),
        name="fetch",
    )(in_hbm(momentum), in_hbm(factor))


def left_kernel(at, m_ref, high_ref, low_ref, out_ref):
    half = high_ref.shape[0] // 2
    total = None
    for k in range(2):
        span = pl.ds(k * half, half)
        piece = m_ref[pl.ds(at, out_ref.shape[0]), span]
        part = dot(three(*split(piece), 1), three_other(high_ref[span, :], low_ref[span, :], 0))
        total = part if total is None else total + part
    out_ref[...] = total


def left_piece(momentum, high, low, at, size):
    cols, rank = high.shape
    return pl.pallas_call(
        lambda *refs: left_kernel(at, *refs),
        in_specs=[VMEM] * 3,
        out_specs=VMEM,
        out_shape=jax.ShapeDtypeStruct((size, rank), F32),
        compiler_params=params(),
        cost_estimate=cost(6 * size * cols * rank, 2**20),
        name="left",
    )(in_vmem(momentum), in_vmem(high), in_vmem(low))


def raw_kernel(at, groups, added, with_gram, order_ref, left_ref, m_ref, *refs):
    count = len(groups) + with_gram
    before_refs, out_refs = refs[: count * added], refs[count * added :]
    left = left_ref[...]
    lhs = three(*split(left.T), 1)
    if with_gram:
        gram = full_dot(left, left, ((0,), (0,)))
        out_refs[-1][...] = before_refs[-1][...] + gram if added else gram
    for g, places in enumerate(groups):
        width = out_refs[g].shape[2]
        for s, place in enumerate(places):
            span = pl.ds(pl.multiple_of(order_ref[place] * width, width), width)
            part = dot(lhs, three_other(*split(m_ref[pl.ds(at, left.shape[0]), span]), 0))
            out_refs[g][s] = before_refs[g][s] + part if added else part


def raw_pieces(order, groups, left, momentum, at, before, with_gram):
    rows, rank = left.shape
    width = momentum.shape[1] // RING
    chunks = sum(len(places) for places in groups)
    shapes = [jax.ShapeDtypeStruct((len(places), rank, width), F32) for places in groups]
    shapes += [jax.ShapeDtypeStruct((rank, rank), F32)] * with_gram
    return pl.pallas_call(
        lambda *refs: raw_kernel(at, groups, bool(before), with_gram, *refs),
        in_specs=[SMEM] + [VMEM] * (2 + len(before)),
        out_specs=[VMEM] * len(shapes),
        out_shape=shapes,
        compiler_params=params(),
        cost_estimate=cost(6 * rows * rank * width * chunks, 2**20),
        name="raw_right",
    )(order, left, in_vmem(momentum), *before)


def gram_kernel(chunks, order_ref, left_ref, before_ref, out_ref):
    left = left_ref[...]
    total = before_ref[...] + full_dot(left, left, ((0,), (0,)))
    half = total.shape[0] // 2
    first = order_ref[0] < chunks
    out_ref[0] = jnp.where(first, total[:half], total[half:])
    out_ref[1] = jnp.where(first, total[half:], total[:half])


def gram_halves(order, left, before):
    rank = left.shape[1]
    return pl.pallas_call(
        lambda *refs: gram_kernel(RING // 2, *refs),
        in_specs=[SMEM, VMEM, VMEM],
        out_specs=VMEM,
        out_shape=jax.ShapeDtypeStruct((2, rank // 2, rank), F32),
        compiler_params=params(),
        cost_estimate=cost(12 * rank * rank * left.shape[0], 2**20),
        name="gram",
    )(order, left, before)


def full_dot(a, b, contract=((1,), (0,))):
    return lax.dot_general(a, b, (contract, ((), ())), precision=HIGHEST, preferred_element_type=F32)


def rough_dot(a, b, contract=((1,), (0,))):
    return lax.dot_general(a.astype(BF16), b.astype(BF16), (contract, ((), ())), preferred_element_type=F32)


def newton(gram_ref, x_ref):
    rank = gram_ref.shape[0]
    rows = lax.broadcasted_iota(jnp.int32, (rank, rank), 0)
    cols = lax.broadcasted_iota(jnp.int32, (rank, rank), 1)
    eye = jnp.where(rows == cols, 1.0, 0.0).astype(F32)
    gram = gram_ref[...]
    x = eye * lax.rsqrt(jnp.sum(gram * eye, axis=1, keepdims=True))
    for times in (rough_dot, rough_dot, full_dot, full_dot):
        error = times(times(x, gram), x, ((1,), (1,))) - eye
        x = x - times(jnp.where(rows > cols, error, 0.5 * eye * error), x)
    x_ref[...] = x
    return jnp.sum(error * error), jnp.min(jnp.where(rows == cols, x, 1.0))


def eliminate(work_ref):
    rank = work_ref.shape[0]
    rows = lax.broadcasted_iota(jnp.int32, (rank, 2 * rank), 0)
    cols = lax.broadcasted_iota(jnp.int32, (rank, 2 * rank), 1)

    def step(j, carry):
        work = work_ref[...]
        row = work_ref[pl.ds(j, 1), :]
        pivot = jnp.sum(jnp.where(cols[:1] == j, row, 0.0), axis=1, keepdims=True)
        column = jnp.sum(jnp.where(cols == j, work, 0.0), axis=1, keepdims=True)
        ratio = jnp.where(rows[:, :1] > j, column * (1.0 / pivot), 0.0)
        work_ref[...] = work - ratio * row
        return carry

    lax.fori_loop(0, rank, step, 0)
    work = work_ref[...]
    pivots = jnp.sum(jnp.where(rows == cols, work, 0.0), axis=1, keepdims=True)
    return jnp.where(rows + rank >= cols, work / jnp.sqrt(pivots), 0.0)[:, rank:]


def factor_kernel(pieces, chunks, order_ref, kept_ref, sent_ref, *refs):
    left_refs = refs[:pieces]
    inv_ref, orth_ref, operand_ref, gram_ref, work_ref = refs[pieces:]
    half, rank = kept_ref.shape
    first = order_ref[0] < chunks
    gram_ref[:half] = jnp.where(first, kept_ref[...], sent_ref[...])
    gram_ref[half:] = jnp.where(first, sent_ref[...], kept_ref[...])
    before, least = newton(gram_ref, inv_ref)

    @pl.when(jnp.logical_not((before < 1e-6) & (least > 0.0)))
    def _():
        rows = lax.broadcasted_iota(jnp.int32, (rank, rank), 0)
        cols = lax.broadcasted_iota(jnp.int32, (rank, rank), 1)
        work_ref[:, :rank] = gram_ref[...]
        work_ref[:, rank:] = jnp.where(rows == cols, 1.0, 0.0).astype(F32)
        inv_ref[...] = eliminate(work_ref)

    inverse = three_other(*split(inv_ref[...]), 1)
    at = 0
    for ref in left_refs:
        size = ref.shape[0]
        orth = lax.dot_general(
            three(*split(ref[...]), 1), inverse, (((1,), (1,)), ((), ())), preferred_element_type=F32
        )
        orth_ref[at : at + size, :] = orth
        operand_ref[at : at + size, :] = three(*split(-0.5 * orth), 1)
        at += size


def factor(order, kept, sent, lefts):
    rank = kept.shape[1]
    rows = sum(x.shape[0] for x in lefts)
    return pl.pallas_call(
        lambda *refs: factor_kernel(len(lefts), RING // 2, *refs),
        in_specs=[SMEM] + [VMEM] * (2 + len(lefts)),
        out_specs=[VMEM] * 3,
        out_shape=[
            jax.ShapeDtypeStruct((rank, rank), F32),
            jax.ShapeDtypeStruct((rows, rank), F32),
            jax.ShapeDtypeStruct((rows, 3 * rank), BF16),
        ],
        scratch_shapes=[pltpu.VMEM((rank, rank), F32), pltpu.VMEM((rank, 2 * rank), F32)],
        compiler_params=params(),
        cost_estimate=cost(1, 1),
        name="factor",
    )(order, kept, sent, *lefts)


def square_kernel(inv_ref, raw_ref, out_ref):
    right = jnp.dot(inv_ref[...], raw_ref[0], precision=HIGHEST, preferred_element_type=F32)
    ones = jnp.ones((8, right.shape[1]), F32)
    out_ref[...] = lax.dot_general(
        ones, right * right, (((1,), (1,)), ((), ())), precision=HIGHEST, preferred_element_type=F32
    )


def square_row(inverse, raw):
    rank = inverse.shape[0]
    return pl.pallas_call(
        square_kernel,
        out_shape=jax.ShapeDtypeStruct((8, rank), F32),
        compiler_params=params(),
        cost_estimate=cost(12 * rank * rank * raw.shape[2], 2**20),
        name="squares",
    )(inverse, raw)


def operand_kernel(count, scale, *refs):
    square_refs = refs[:count]
    orth_ref, operand_ref = refs[count:]
    squares = square_refs[0][...]
    for ref in square_refs[1:]:
        squares = squares + ref[...]
    norm = scale / jnp.sqrt(squares[:1] + 1e-06)
    operand_ref[...] = three(*split(orth_ref[...] * norm), 1)


def update_operand(squares, orth, scale):
    rows, rank = orth.shape
    return pl.pallas_call(
        lambda *refs: operand_kernel(len(squares), scale, *refs),
        out_shape=jax.ShapeDtypeStruct((rows, 3 * rank), BF16),
        compiler_params=params(),
        cost_estimate=cost(rows * rank * 10, rows * rank * 12),
        name="operand",
    )(*squares, orth)


def new_kernel(places, chained, order_ref, operand_ref, inv_ref, m_ref, *refs):
    count = len(places)
    raw_refs, refs = refs[:count], refs[count + chained :]
    out_hbm, right_refs, (out_ref, sem) = refs[0], refs[1 : 1 + count], refs[1 + count :]
    _, rows, width = out_ref.shape
    parts = sem.shape[1]
    tile = rows // parts
    inverse = three(*split(inv_ref[...]), 1)
    for raw_ref, right_ref in zip(raw_refs, right_refs):
        right = dot(inverse, three_other(*split(raw_ref[0]), 0))
        right_ref[...] = three_other(*split(right), 0)
    copies = []
    for s, right_ref in enumerate(right_refs):
        span = pl.ds(pl.multiple_of(order_ref[places[s]] * width, width), width)
        right = right_ref[...]
        for part in range(parts):
            at = pl.ds(part * tile, tile)
            out_ref[s, at] = m_ref[at, span] + dot(operand_ref[at, :], right)
            copies.append(pltpu.make_async_copy(out_ref.at[s, at], out_hbm.at[at, span], sem.at[s, part]))
            copies[-1].start()
    for copy in copies:
        copy.wait()


def new_chunks(order, places, operand, inverse, raws, momentum, before):
    rows, cols = momentum.shape
    _, rank, width = raws[0].shape
    count, parts = len(raws), 4
    outs = pl.pallas_call(
        lambda *refs: new_kernel(places, len(before), *refs),
        in_specs=[SMEM] + [VMEM] * (3 + count) + [HBM] * len(before),
        out_specs=[HBM] + [VMEM] * count,
        out_shape=[jax.ShapeDtypeStruct((rows, cols), F32)]
        + [jax.ShapeDtypeStruct((3 * rank, width), BF16)] * count,
        scratch_shapes=[pltpu.VMEM((count, rows, width), F32), pltpu.SemaphoreType.DMA((count, parts))],
        input_output_aliases={4 + count: 0} if before else {},
        compiler_params=params(),
        cost_estimate=cost(6 * count * rows * rank * width, 4 * count * rows * width),
        name="new_momentum",
    )(order, operand, inverse, in_vmem(momentum), *raws, *before)
    return [outs[0]], list(outs[1:])


def update_kernel(places, chained, order_ref, operand_ref, *refs):
    count = len(places)
    right_refs, (out_hbm, out_ref, sem) = refs[:count], refs[count + chained :]
    _, rows, width = out_ref.shape
    parts = sem.shape[1]
    tile = rows // parts
    copies = []
    for s, right_ref in enumerate(right_refs):
        span = pl.ds(pl.multiple_of(order_ref[places[s]] * width, width), width)
        right = right_ref[...]
        for part in range(parts):
            at = pl.ds(part * tile, tile)
            out_ref[s, at] = dot(operand_ref[at, :], right)
            copies.append(pltpu.make_async_copy(out_ref.at[s, at], out_hbm.at[at, span], sem.at[s, part]))
            copies[-1].start()
    for copy in copies:
        copy.wait()


def update_chunks(order, places, operand, rights, before, cols):
    rows = operand.shape[0]
    width = rights[0].shape[1]
    rank = rights[0].shape[0] // 3
    count, parts = len(rights), 4
    return [
        pl.pallas_call(
            lambda *refs: update_kernel(places, len(before), *refs),
            in_specs=[SMEM] + [VMEM] * (1 + count) + [HBM] * len(before),
            out_specs=HBM,
            out_shape=jax.ShapeDtypeStruct((rows, cols), F32),
            scratch_shapes=[pltpu.VMEM((count, rows, width), F32), pltpu.SemaphoreType.DMA((count, parts))],
            input_output_aliases={2 + count: 0} if before else {},
            compiler_params=params(),
            cost_estimate=cost(6 * count * rows * rank * width, 4 * count * rows * width),
            name="update",
        )(order, operand, *rights, *before)
    ]


def add_kernel(*refs):
    refs[-1][...] = sum((ref[...] for ref in refs[1:-1]), refs[0][...])


def add(*values):
    return pl.pallas_call(
        add_kernel,
        in_specs=[VMEM] * len(values),
        out_specs=VMEM,
        out_shape=jax.ShapeDtypeStruct(values[0].shape, F32),
        compiler_params=params(),
        cost_estimate=cost(values[0].size, 1),
        name="add",
    )(*values)


def half_kernel(*refs):
    *value_refs, second_ref, first_ref = refs
    half = first_ref.shape[0]
    second_ref[...] = sum((ref[half:] for ref in value_refs[1:]), value_refs[0][half:])
    first_ref[...] = sum((ref[:half] for ref in value_refs[1:]), value_refs[0][:half])


def add_halves(*values):
    half = values[0].shape[0] // 2
    shape = jax.ShapeDtypeStruct((half, *values[0].shape[1:]), F32)
    return pl.pallas_call(
        half_kernel,
        in_specs=[VMEM] * len(values),
        out_specs=[VMEM] * 2,
        out_shape=[shape] * 2,
        compiler_params=params(),
        cost_estimate=cost(values[0].size, 1),
        name="add_halves",
    )(*values)


def choose_kernel(order_ref, a_ref, b_ref, out_ref):
    out_ref[...] = jnp.where(order_ref[RING] > 0, a_ref[...], b_ref[...])


def choose(order, a, b):
    return pl.pallas_call(
        choose_kernel,
        in_specs=[SMEM, VMEM, VMEM],
        out_specs=VMEM,
        out_shape=jax.ShapeDtypeStruct(a.shape, F32),
        compiler_params=params(),
        cost_estimate=cost(a.size, 1),
        name="choose",
    )(order, a, b)


PAIR = [(r, r ^ 1) for r in range(RING)]
NEAR = [(r, r ^ (2 if r % 2 == 0 else 4)) for r in range(RING)]
FAR = [(r, r ^ (4 if r % 2 == 0 else 2)) for r in range(RING)]
ACROSS = [(r, r ^ 6) for r in range(RING)]


def along(x, pairs):
    return lax.ppermute(x, "row", pairs)


def together(*values):
    return lax.optimization_barrier(values)


def local(momentum, right_factor, scale):
    rows, cols = momentum.shape
    me, at = lax.axis_index("row"), lax.axis_index("col")
    core, first, second = me % 2, me // 2 % 2, me // 4
    low_id = jnp.where(core == 0, 2 * first + second, 2 * second + first)
    pair_id = jnp.where(core == 0, 2 * second + first, 2 * first + second)
    slots = jnp.arange(RING + 1, dtype=jnp.int32)
    order = jnp.where(slots < 4, 4 * core + (slots ^ low_id), 4 * (1 - core) + ((slots - 4) ^ pair_id))
    order = jnp.where(slots < RING, order, (at > 0) & (at < LINE - 1)).astype(jnp.int32)
    order, right_factor = together(order, right_factor)

    size = rows // 4
    resident, high, low = fetch(momentum, right_factor)

    def left_of(k, high):
        return left_piece(resident, high, low, k * size, size)

    def inward(x):
        return lax.ppermute(x, "col", [(0, 1), (3, 2)])

    def across(x):
        return lax.ppermute(x, "col", [(1, 2), (2, 1)])

    def outward(x):
        return lax.ppermute(x, "col", [(1, 0), (2, 3)])

    parts = [left_of(k, high) for k in range(3)]
    held = [add(part, inward(part)) for part in parts]
    high, held[0] = together(high, held[0])
    part = left_of(3, high)
    held.append(add(part, inward(part)))
    crossed = [add(x, across(x)) for x in held[:3]]
    held[3], crossed[0] = together(held[3], crossed[0])
    crossed.append(add(held[3], across(held[3])))
    lefts = [choose(order, x, outward(x)) for x in crossed]

    groups = ((7, 6), (3, 2), (5, 4), (1, 0))
    sums = []
    for k in range(3):
        sums = raw_pieces(order, groups, lefts[k], resident, k * size, sums, 1)
    *sums, gram = sums

    def last(order, g):
        return raw_pieces(order, groups[g : g + 1], lefts[3], resident, 3 * size, [sums[g]], 0)[0]

    sent_far = last(order, 0)
    order_1, sent_far = together(order, sent_far)
    halves = gram_halves(order_1, lefts[3], gram)
    order_2, halves = together(order_1, halves)
    kept_far = last(order_2, 1)
    kept_far = add(kept_far, along(sent_far, PAIR))
    got_near = along(kept_far, NEAR)
    kept = add(halves[0], along(halves[1], PAIR))
    order_3, kept_far, kept = together(order_2, kept_far, kept)
    sent_near, kept_near = last(order_3, 2), last(order_3, 3)
    kept = add(kept, *[along(kept, pairs) for pairs in (NEAR, FAR, ACROSS)])
    got_near, kept = together(got_near, kept)
    slot_0, slot_1 = add_halves(kept_near, along(sent_near, PAIR), got_near)
    got_own = along(slot_1, FAR)
    inverse, orth, operand = factor(order, kept, along(kept, PAIR), lefts)
    got_own, inverse = together(got_own, inverse)
    own = add(slot_0, got_own)

    def new_pair(slot, raws, before):
        return new_chunks(order, (slot, slot + 4), operand, inverse, raws, resident, before)

    chunk_1, pair = along(own, FAR), along(own, PAIR)
    squares = square_row(inverse, own)
    squares = add(squares, along(squares, PAIR))
    squares, again = together(squares, own)
    got, chunk_2 = along(squares, NEAR), along(again, NEAR)
    new, rights = new_chunks(order, (0, 4), operand, inverse, [own, pair], resident, [])
    got, chunk_1, new[0] = together(got, chunk_1, new[0])
    chunk_3, pair_1 = along(chunk_1, NEAR), along(chunk_1, PAIR)
    squares = add(squares, got)
    got = along(squares, FAR)
    pair_1, chunk_2 = together(pair_1, chunk_2)
    new, right = new_chunks(order, (1, 5), operand, inverse, [chunk_1, pair_1], resident, new)
    rights += right
    got, chunk_2, chunk_3, new[0] = together(got, chunk_2, chunk_3, new[0])
    pair_2, pair_3 = along(chunk_2, PAIR), along(chunk_3, PAIR)
    squares = add(squares, got)
    gots = [lax.ppermute(squares, "col", [(c, c ^ d) for c in range(LINE)]) for d in range(1, LINE)]
    *gots, new[0] = together(*gots, new[0])
    raws = [chunk_2, pair_2, chunk_3, pair_3]
    new, right = new_chunks(order, (2, 6, 3, 7), operand, inverse, raws, resident, new)
    rights += right
    scaled = update_operand([squares] + gots, orth, scale)
    update = update_chunks(order, (0, 4, 1, 5, 2, 6, 3, 7), scaled, rights, [], cols)
    return new[0], update[0]


def general(momentum, right_factor, scale):
    left = lax.psum(jnp.dot(momentum, right_factor, precision=HIGHEST), "col")
    gram_part = jnp.dot(left.T, left, precision=HIGHEST)
    raw_part = jnp.dot(left.T, momentum, precision=HIGHEST)
    gram, raw = lax.psum((gram_part, raw_part), "row")
    lower = jnp.linalg.cholesky(gram)
    orth = jax.scipy.linalg.solve_triangular(lower, left.T, lower=True).T
    right = jax.scipy.linalg.solve_triangular(lower, raw, lower=True)
    squares = lax.psum(jnp.sum(right * right, axis=1, keepdims=True), "col")
    factor_q = right / jnp.sqrt(squares + 1e-06)
    new = momentum - 0.5 * jnp.dot(orth, right, precision=HIGHEST)
    return new, scale * jnp.dot(orth, factor_q, precision=HIGHEST)


def solution(mesh):
    by_hand = mesh.shape["row"] == RING and mesh.shape["col"] == LINE
    program = local if by_hand else general

    def run(momentum, right_factor):
        rows, cols = momentum.shape
        scale = math.sqrt(rows * cols / right_factor.shape[1])
        return jax.shard_map(
            lambda m, q: program(m, q, scale),
            mesh=mesh,
            in_specs=(P("row", "col"), P("col", None)),
            out_specs=(P("row", "col"), P("row", "col")),
            check_vma=False,
        )(momentum, right_factor)

    return run
```

```python
import math

import jax
import jax.numpy as jnp
from jax import lax
from jax.experimental import pallas as pl
from jax.experimental.pallas import tpu as pltpu
from jax.sharding import PartitionSpec as P

F32 = jnp.float32
BF16 = jnp.bfloat16
HIGHEST = lax.Precision.HIGHEST
VMEM_LIMIT = 20 * 1024 * 1024
SMEM = pl.BlockSpec(memory_space=pltpu.SMEM)
VMEM = pl.BlockSpec(memory_space=pltpu.VMEM)
HBM = pl.BlockSpec(memory_space=pltpu.HBM)
ANY = pl.BlockSpec(memory_space=pl.ANY)
LINE = 4
RING = 8
SHARES = (3, 3, 2)


def split(x):
    high = x.astype(BF16)
    return high, (x - high.astype(F32)).astype(BF16)


def dot(a, b):
    return jnp.dot(a, b, preferred_element_type=F32)


def params():
    return pltpu.CompilerParams(vmem_limit_bytes=VMEM_LIMIT)


def cost(flops, bytes_accessed):
    return pl.CostEstimate(flops=int(flops), bytes_accessed=int(bytes_accessed), transcendentals=0)


def in_vmem(x):
    return pltpu.with_memory_space_constraint(x, pltpu.VMEM)


def in_hbm(x):
    return pltpu.with_memory_space_constraint(x, pltpu.HBM)


def three(high, low, axis):
    return jnp.concatenate([high, high, low], axis=axis)


def three_other(high, low, axis):
    return jnp.concatenate([high, low, high], axis=axis)


def fetch_kernel(m_hbm, q_hbm, m_ref, high_ref, low_ref, q_ref, m_sem, q_sem):
    half = q_ref.shape[0] // 2
    spans = [pl.ds(k * half, half) for k in range(2)]
    copies = [pltpu.make_async_copy(q_hbm.at[span], q_ref.at[span], q_sem.at[k]) for k, span in enumerate(spans)]
    whole = pltpu.make_async_copy(m_hbm, m_ref, m_sem)
    for copy in copies:
        copy.start()
    whole.start()
    for copy, span in zip(copies, spans):
        copy.wait()
        high_ref[span, :], low_ref[span, :] = split(q_ref[span, :])
    whole.wait()


def fetch(momentum, factor):
    cols, rank = factor.shape
    return pl.pallas_call(
        fetch_kernel,
        in_specs=[HBM, HBM],
        out_specs=[ANY, VMEM, VMEM],
        out_shape=[
            pltpu.VMEM(momentum.shape, F32),
            pltpu.VMEM((cols, rank), BF16),
            pltpu.VMEM((cols, rank), BF16),
        ],
        scratch_shapes=[pltpu.VMEM((cols, rank), F32), pltpu.SemaphoreType.DMA, pltpu.SemaphoreType.DMA((2,))],
        compiler_params=params(),
        cost_estimate=cost(cols * rank, 4 * cols * (momentum.shape[0] + rank)),
        name="fetch",
    )(in_hbm(momentum), in_hbm(factor))


def left_kernel(at, m_ref, high_ref, low_ref, out_ref):
    half = high_ref.shape[0] // 2
    total = None
    for k in range(2):
        span = pl.ds(k * half, half)
        piece = m_ref[pl.ds(at, out_ref.shape[0]), span]
        part = dot(three(*split(piece), 1), three_other(high_ref[span, :], low_ref[span, :], 0))
        total = part if total is None else total + part
    out_ref[...] = total


def left_piece(momentum, high, low, at, size):
    cols, rank = high.shape
    return pl.pallas_call(
        lambda *refs: left_kernel(at, *refs),
        in_specs=[VMEM] * 3,
        out_specs=VMEM,
        out_shape=jax.ShapeDtypeStruct((size, rank), F32),
        compiler_params=params(),
        cost_estimate=cost(6 * size * cols * rank, 2**20),
        name="left",
    )(in_vmem(momentum), in_vmem(high), in_vmem(low))


def raw_kernel(at, groups, added, with_gram, order_ref, left_ref, m_ref, *refs):
    count = len(groups) + with_gram
    before_refs, out_refs = refs[: count * added], refs[count * added :]
    left = left_ref[...]
    lhs = three(*split(left.T), 1)
    if with_gram:
        gram = full_dot(left, left, ((0,), (0,)))
        out_refs[-1][...] = before_refs[-1][...] + gram if added else gram
    for g, places in enumerate(groups):
        width = out_refs[g].shape[2]
        for s, place in enumerate(places):
            span = pl.ds(pl.multiple_of(order_ref[place] * width, width), width)
            part = dot(lhs, three_other(*split(m_ref[pl.ds(at, left.shape[0]), span]), 0))
            out_refs[g][s] = before_refs[g][s] + part if added else part


def raw_pieces(order, groups, left, momentum, at, before, with_gram):
    rows, rank = left.shape
    width = momentum.shape[1] // RING
    chunks = sum(len(places) for places in groups)
    shapes = [jax.ShapeDtypeStruct((len(places), rank, width), F32) for places in groups]
    shapes += [jax.ShapeDtypeStruct((rank, rank), F32)] * with_gram
    return pl.pallas_call(
        lambda *refs: raw_kernel(at, groups, bool(before), with_gram, *refs),
        in_specs=[SMEM] + [VMEM] * (2 + len(before)),
        out_specs=[VMEM] * len(shapes),
        out_shape=shapes,
        compiler_params=params(),
        cost_estimate=cost(6 * rows * rank * width * chunks, 2**20),
        name="raw_right",
    )(order, left, in_vmem(momentum), *before)


def gram_kernel(chunks, order_ref, left_ref, before_ref, out_ref):
    left = left_ref[...]
    total = before_ref[...] + full_dot(left, left, ((0,), (0,)))
    half = total.shape[0] // 2
    first = order_ref[0] < chunks
    out_ref[0] = jnp.where(first, total[:half], total[half:])
    out_ref[1] = jnp.where(first, total[half:], total[:half])


def gram_halves(order, left, before):
    rank = left.shape[1]
    return pl.pallas_call(
        lambda *refs: gram_kernel(RING // 2, *refs),
        in_specs=[SMEM, VMEM, VMEM],
        out_specs=VMEM,
        out_shape=jax.ShapeDtypeStruct((2, rank // 2, rank), F32),
        compiler_params=params(),
        cost_estimate=cost(12 * rank * rank * left.shape[0], 2**20),
        name="gram",
    )(order, left, before)


def full_dot(a, b, contract=((1,), (0,))):
    return lax.dot_general(a, b, (contract, ((), ())), precision=HIGHEST, preferred_element_type=F32)


def rough_dot(a, b, contract=((1,), (0,))):
    return lax.dot_general(a.astype(BF16), b.astype(BF16), (contract, ((), ())), preferred_element_type=F32)


def split_dot(a, b, contract=((1,), (0,))):
    (a_high, a_low), (b_high, b_low) = split(a), split(b)
    return rough_dot(a_high, b_high, contract) + rough_dot(a_high, b_low, contract) + rough_dot(a_low, b_high, contract)


def newton(gram_ref, x_ref):
    rank = gram_ref.shape[0]
    rows = lax.broadcasted_iota(jnp.int32, (rank, rank), 0)
    cols = lax.broadcasted_iota(jnp.int32, (rank, rank), 1)
    eye = jnp.where(rows == cols, 1.0, 0.0).astype(F32)
    gram = gram_ref[...]
    x = eye * lax.rsqrt(jnp.sum(gram * eye, axis=1, keepdims=True))
    for times in (rough_dot, rough_dot, split_dot, full_dot):
        error = times(times(x, gram), x, ((1,), (1,))) - eye
        x = x - times(jnp.where(rows > cols, error, 0.5 * eye * error), x)
    x_ref[...] = x
    return jnp.sum(error * error), jnp.min(jnp.where(rows == cols, x, 1.0))


def eliminate(work_ref):
    rank = work_ref.shape[0]
    rows = lax.broadcasted_iota(jnp.int32, (rank, 2 * rank), 0)
    cols = lax.broadcasted_iota(jnp.int32, (rank, 2 * rank), 1)

    def step(j, carry):
        work = work_ref[...]
        row = work_ref[pl.ds(j, 1), :]
        pivot = jnp.sum(jnp.where(cols[:1] == j, row, 0.0), axis=1, keepdims=True)
        column = jnp.sum(jnp.where(cols == j, work, 0.0), axis=1, keepdims=True)
        ratio = jnp.where(rows[:, :1] > j, column * (1.0 / pivot), 0.0)
        work_ref[...] = work - ratio * row
        return carry

    lax.fori_loop(0, rank, step, 0)
    work = work_ref[...]
    pivots = jnp.sum(jnp.where(rows == cols, work, 0.0), axis=1, keepdims=True)
    return jnp.where(rows + rank >= cols, work / jnp.sqrt(pivots), 0.0)[:, rank:]


def factor_kernel(pieces, chunks, order_ref, kept_ref, sent_ref, *refs):
    left_refs = refs[:pieces]
    inv_ref, orth_ref, operand_ref, gram_ref, work_ref = refs[pieces:]
    half, rank = kept_ref.shape
    first = order_ref[0] < chunks
    gram_ref[:half] = jnp.where(first, kept_ref[...], sent_ref[...])
    gram_ref[half:] = jnp.where(first, sent_ref[...], kept_ref[...])
    before, least = newton(gram_ref, inv_ref)

    @pl.when(jnp.logical_not((before < 1e-6) & (least > 0.0)))
    def _():
        rows = lax.broadcasted_iota(jnp.int32, (rank, rank), 0)
        cols = lax.broadcasted_iota(jnp.int32, (rank, rank), 1)
        work_ref[:, :rank] = gram_ref[...]
        work_ref[:, rank:] = jnp.where(rows == cols, 1.0, 0.0).astype(F32)
        inv_ref[...] = eliminate(work_ref)

    inverse = three_other(*split(inv_ref[...]), 1)
    at = 0
    for ref in left_refs:
        size = ref.shape[0]
        orth = lax.dot_general(
            three(*split(ref[...]), 1), inverse, (((1,), (1,)), ((), ())), preferred_element_type=F32
        )
        orth_ref[at : at + size, :] = orth
        operand_ref[at : at + size, :] = three(*split(-0.5 * orth), 1)
        at += size


def factor(order, kept, sent, lefts):
    rank = kept.shape[1]
    rows = sum(x.shape[0] for x in lefts)
    return pl.pallas_call(
        lambda *refs: factor_kernel(len(lefts), RING // 2, *refs),
        in_specs=[SMEM] + [VMEM] * (2 + len(lefts)),
        out_specs=[VMEM] * 3,
        out_shape=[
            jax.ShapeDtypeStruct((rank, rank), F32),
            jax.ShapeDtypeStruct((rows, rank), F32),
            jax.ShapeDtypeStruct((rows, 3 * rank), BF16),
        ],
        scratch_shapes=[pltpu.VMEM((rank, rank), F32), pltpu.VMEM((rank, 2 * rank), F32)],
        compiler_params=params(),
        cost_estimate=cost(1, 1),
        name="factor",
    )(order, kept, sent, *lefts)


def square_kernel(inv_ref, raw_ref, out_ref):
    right = jnp.dot(inv_ref[...], raw_ref[0], precision=HIGHEST, preferred_element_type=F32)
    ones = jnp.ones((8, right.shape[1]), F32)
    out_ref[...] = lax.dot_general(
        ones, right * right, (((1,), (1,)), ((), ())), precision=HIGHEST, preferred_element_type=F32
    )


def square_row(inverse, raw):
    rank = inverse.shape[0]
    return pl.pallas_call(
        square_kernel,
        out_shape=jax.ShapeDtypeStruct((8, rank), F32),
        compiler_params=params(),
        cost_estimate=cost(12 * rank * rank * raw.shape[2], 2**20),
        name="squares",
    )(inverse, raw)


def operand_kernel(count, scale, *refs):
    square_refs = refs[:count]
    orth_ref, operand_ref = refs[count:]
    squares = square_refs[0][...]
    for ref in square_refs[1:]:
        squares = squares + ref[...]
    norm = scale / jnp.sqrt(squares[:1] + 1e-06)
    operand_ref[...] = three(*split(orth_ref[...] * norm), 1)


def update_operand(squares, orth, scale):
    rows, rank = orth.shape
    return pl.pallas_call(
        lambda *refs: operand_kernel(len(squares), scale, *refs),
        out_shape=jax.ShapeDtypeStruct((rows, 3 * rank), BF16),
        compiler_params=params(),
        cost_estimate=cost(rows * rank * 10, rows * rank * 12),
        name="operand",
    )(*squares, orth)


def new_kernel(places, chained, order_ref, operand_ref, inv_ref, m_ref, *refs):
    count = len(places)
    raw_refs, refs = refs[:count], refs[count + chained :]
    out_hbm, right_refs, (out_ref, sem) = refs[0], refs[1 : 1 + count], refs[1 + count :]
    _, rows, width = out_ref.shape
    parts = sem.shape[1]
    tile = rows // parts
    inverse = three(*split(inv_ref[...]), 1)
    for raw_ref, right_ref in zip(raw_refs, right_refs):
        right = dot(inverse, three_other(*split(raw_ref[0]), 0))
        right_ref[...] = three_other(*split(right), 0)
    copies = []
    for s, right_ref in enumerate(right_refs):
        span = pl.ds(pl.multiple_of(order_ref[places[s]] * width, width), width)
        right = right_ref[...]
        for part in range(parts):
            at = pl.ds(part * tile, tile)
            out_ref[s, at] = m_ref[at, span] + dot(operand_ref[at, :], right)
            copies.append(pltpu.make_async_copy(out_ref.at[s, at], out_hbm.at[at, span], sem.at[s, part]))
            copies[-1].start()
    for copy in copies:
        copy.wait()


def new_chunks(order, places, operand, inverse, raws, momentum, before):
    rows, cols = momentum.shape
    _, rank, width = raws[0].shape
    count, parts = len(raws), 4
    outs = pl.pallas_call(
        lambda *refs: new_kernel(places, len(before), *refs),
        in_specs=[SMEM] + [VMEM] * (3 + count) + [HBM] * len(before),
        out_specs=[HBM] + [VMEM] * count,
        out_shape=[jax.ShapeDtypeStruct((rows, cols), F32)]
        + [jax.ShapeDtypeStruct((3 * rank, width), BF16)] * count,
        scratch_shapes=[pltpu.VMEM((count, rows, width), F32), pltpu.SemaphoreType.DMA((count, parts))],
        input_output_aliases={4 + count: 0} if before else {},
        compiler_params=params(),
        cost_estimate=cost(6 * count * rows * rank * width, 4 * count * rows * width),
        name="new_momentum",
    )(order, operand, inverse, in_vmem(momentum), *raws, *before)
    return [outs[0]], list(outs[1:])


def update_kernel(places, chained, order_ref, operand_ref, *refs):
    count = len(places)
    right_refs, (out_hbm, out_ref, sem) = refs[:count], refs[count + chained :]
    _, rows, width = out_ref.shape
    parts = sem.shape[1]
    tile = rows // parts
    copies = []
    for s, right_ref in enumerate(right_refs):
        span = pl.ds(pl.multiple_of(order_ref[places[s]] * width, width), width)
        right = right_ref[...]
        for part in range(parts):
            at = pl.ds(part * tile, tile)
            out_ref[s, at] = dot(operand_ref[at, :], right)
            copies.append(pltpu.make_async_copy(out_ref.at[s, at], out_hbm.at[at, span], sem.at[s, part]))
            copies[-1].start()
    for copy in copies:
        copy.wait()


def update_chunks(order, places, operand, rights, before, cols):
    rows = operand.shape[0]
    width = rights[0].shape[1]
    rank = rights[0].shape[0] // 3
    count, parts = len(rights), 4
    return [
        pl.pallas_call(
            lambda *refs: update_kernel(places, len(before), *refs),
            in_specs=[SMEM] + [VMEM] * (1 + count) + [HBM] * len(before),
            out_specs=HBM,
            out_shape=jax.ShapeDtypeStruct((rows, cols), F32),
            scratch_shapes=[pltpu.VMEM((count, rows, width), F32), pltpu.SemaphoreType.DMA((count, parts))],
            input_output_aliases={2 + count: 0} if before else {},
            compiler_params=params(),
            cost_estimate=cost(6 * count * rows * rank * width, 4 * count * rows * width),
            name="update",
        )(order, operand, *rights, *before)
    ]


def add_kernel(*refs):
    refs[-1][...] = sum((ref[...] for ref in refs[1:-1]), refs[0][...])


def add(*values):
    return pl.pallas_call(
        add_kernel,
        in_specs=[VMEM] * len(values),
        out_specs=VMEM,
        out_shape=jax.ShapeDtypeStruct(values[0].shape, F32),
        compiler_params=params(),
        cost_estimate=cost(values[0].size, 1),
        name="add",
    )(*values)


def half_kernel(*refs):
    *value_refs, second_ref, first_ref = refs
    half = first_ref.shape[0]
    second_ref[...] = sum((ref[half:] for ref in value_refs[1:]), value_refs[0][half:])
    first_ref[...] = sum((ref[:half] for ref in value_refs[1:]), value_refs[0][:half])


def add_halves(*values):
    half = values[0].shape[0] // 2
    shape = jax.ShapeDtypeStruct((half, *values[0].shape[1:]), F32)
    return pl.pallas_call(
        half_kernel,
        in_specs=[VMEM] * len(values),
        out_specs=[VMEM] * 2,
        out_shape=[shape] * 2,
        compiler_params=params(),
        cost_estimate=cost(values[0].size, 1),
        name="add_halves",
    )(*values)


def choose_kernel(order_ref, a_ref, b_ref, out_ref):
    out_ref[...] = jnp.where(order_ref[RING] > 0, a_ref[...], b_ref[...])


def choose(order, a, b):
    return pl.pallas_call(
        choose_kernel,
        in_specs=[SMEM, VMEM, VMEM],
        out_specs=VMEM,
        out_shape=jax.ShapeDtypeStruct(a.shape, F32),
        compiler_params=params(),
        cost_estimate=cost(a.size, 1),
        name="choose",
    )(order, a, b)


PAIR = [(r, r ^ 1) for r in range(RING)]
NEAR = [(r, r ^ (2 if r % 2 == 0 else 4)) for r in range(RING)]
FAR = [(r, r ^ (4 if r % 2 == 0 else 2)) for r in range(RING)]
ACROSS = [(r, r ^ 6) for r in range(RING)]


def along(x, pairs):
    return lax.ppermute(x, "row", pairs)


def together(*values):
    return lax.optimization_barrier(values)


def local(momentum, right_factor, scale):
    rows, cols = momentum.shape
    me, at = lax.axis_index("row"), lax.axis_index("col")
    core, first, second = me % 2, me // 2 % 2, me // 4
    low_id = jnp.where(core == 0, 2 * first + second, 2 * second + first)
    pair_id = jnp.where(core == 0, 2 * second + first, 2 * first + second)
    slots = jnp.arange(RING + 1, dtype=jnp.int32)
    order = jnp.where(slots < 4, 4 * core + (slots ^ low_id), 4 * (1 - core) + ((slots - 4) ^ pair_id))
    order = jnp.where(slots < RING, order, (at > 0) & (at < LINE - 1)).astype(jnp.int32)
    order, right_factor = together(order, right_factor)

    resident, high, low = fetch(momentum, right_factor)
    sizes = [rows // 8 * share for share in SHARES]
    starts = [sum(sizes[:k]) for k in range(len(sizes))]

    def left_of(k, high):
        return left_piece(resident, high, low, starts[k], sizes[k])

    def inward(x):
        return lax.ppermute(x, "col", [(0, 1), (3, 2)])

    def across(x):
        return lax.ppermute(x, "col", [(1, 2), (2, 1)])

    def outward(x):
        return lax.ppermute(x, "col", [(1, 0), (2, 3)])

    *early, final = range(len(sizes))
    parts = [left_of(k, high) for k in early]
    held = [add(part, inward(part)) for part in parts]
    high, held[0] = together(high, held[0])
    part = left_of(final, high)
    held.append(add(part, inward(part)))
    crossed = [add(x, across(x)) for x in held[:-1]]
    held[-1], crossed[0] = together(held[-1], crossed[0])
    crossed.append(add(held[-1], across(held[-1])))
    lefts = [choose(order, x, outward(x)) for x in crossed]

    groups = ((7, 6), (3, 2), (5, 4), (1, 0))
    sums = []
    for k in early:
        sums = raw_pieces(order, groups, lefts[k], resident, starts[k], sums, 1)
    *sums, gram = sums

    def last(order, g):
        return raw_pieces(order, groups[g : g + 1], lefts[-1], resident, starts[-1], [sums[g]], 0)[0]

    sent_far = last(order, 0)
    order_1, sent_far = together(order, sent_far)
    halves = gram_halves(order_1, lefts[-1], gram)
    order_2, halves = together(order_1, halves)
    kept_far = last(order_2, 1)
    kept_far = add(kept_far, along(sent_far, PAIR))
    got_near = along(kept_far, NEAR)
    kept = add(halves[0], along(halves[1], PAIR))
    order_3, kept_far, kept = together(order_2, kept_far, kept)
    sent_near, kept_near = last(order_3, 2), last(order_3, 3)
    kept = add(kept, *[along(kept, pairs) for pairs in (NEAR, FAR, ACROSS)])
    got_near, kept = together(got_near, kept)
    slot_0, slot_1 = add_halves(kept_near, along(sent_near, PAIR), got_near)
    got_own = along(slot_1, FAR)
    inverse, orth, operand = factor(order, kept, along(kept, PAIR), lefts)
    got_own, inverse = together(got_own, inverse)
    own = add(slot_0, got_own)

    def new_pair(slot, raws, before):
        return new_chunks(order, (slot, slot + 4), operand, inverse, raws, resident, before)

    chunk_1, pair = along(own, FAR), along(own, PAIR)
    squares = square_row(inverse, own)
    squares = add(squares, along(squares, PAIR))
    squares, again = together(squares, own)
    got, chunk_2 = along(squares, NEAR), along(again, NEAR)
    new, rights = new_chunks(order, (0, 4), operand, inverse, [own, pair], resident, [])
    got, chunk_1, new[0] = together(got, chunk_1, new[0])
    chunk_3, pair_1 = along(chunk_1, NEAR), along(chunk_1, PAIR)
    squares = add(squares, got)
    got = along(squares, FAR)
    pair_1, chunk_2 = together(pair_1, chunk_2)
    new, right = new_chunks(order, (1, 5), operand, inverse, [chunk_1, pair_1], resident, new)
    rights += right
    got, chunk_2, chunk_3, new[0] = together(got, chunk_2, chunk_3, new[0])
    pair_2, pair_3 = along(chunk_2, PAIR), along(chunk_3, PAIR)
    squares = add(squares, got)
    gots = [lax.ppermute(squares, "col", [(c, c ^ d) for c in range(LINE)]) for d in range(1, LINE)]
    *gots, new[0] = together(*gots, new[0])
    raws = [chunk_2, pair_2, chunk_3, pair_3]
    new, right = new_chunks(order, (2, 6, 3, 7), operand, inverse, raws, resident, new)
    rights += right
    scaled = update_operand([squares] + gots, orth, scale)
    update = update_chunks(order, (0, 4, 1, 5, 2, 6, 3, 7), scaled, rights, [], cols)
    return new[0], update[0]


def general(momentum, right_factor, scale):
    left = lax.psum(jnp.dot(momentum, right_factor, precision=HIGHEST), "col")
    gram_part = jnp.dot(left.T, left, precision=HIGHEST)
    raw_part = jnp.dot(left.T, momentum, precision=HIGHEST)
    gram, raw = lax.psum((gram_part, raw_part), "row")
    lower = jnp.linalg.cholesky(gram)
    orth = jax.scipy.linalg.solve_triangular(lower, left.T, lower=True).T
    right = jax.scipy.linalg.solve_triangular(lower, raw, lower=True)
    squares = lax.psum(jnp.sum(right * right, axis=1, keepdims=True), "col")
    factor_q = right / jnp.sqrt(squares + 1e-06)
    new = momentum - 0.5 * jnp.dot(orth, right, precision=HIGHEST)
    return new, scale * jnp.dot(orth, factor_q, precision=HIGHEST)


def solution(mesh):
    by_hand = mesh.shape["row"] == RING and mesh.shape["col"] == LINE
    program = local if by_hand else general

    def run(momentum, right_factor):
        rows, cols = momentum.shape
        scale = math.sqrt(rows * cols / right_factor.shape[1])
        return jax.shard_map(
            lambda m, q: program(m, q, scale),
            mesh=mesh,
            in_specs=(P("row", "col"), P("col", None)),
            out_specs=(P("row", "col"), P("row", "col")),
            check_vma=False,
        )(momentum, right_factor)

    return run
```

```python
import math

import jax
import jax.numpy as jnp
from jax import lax
from jax.experimental import pallas as pl
from jax.experimental.pallas import tpu as pltpu
from jax.sharding import PartitionSpec as P

F32 = jnp.float32
BF16 = jnp.bfloat16
HIGHEST = lax.Precision.HIGHEST
VMEM_LIMIT = 20 * 1024 * 1024
SMEM = pl.BlockSpec(memory_space=pltpu.SMEM)
VMEM = pl.BlockSpec(memory_space=pltpu.VMEM)
HBM = pl.BlockSpec(memory_space=pltpu.HBM)
ANY = pl.BlockSpec(memory_space=pl.ANY)
LINE = 4
RING = 8
SHARES = (3, 3, 2)


def split(x):
    high = x.astype(BF16)
    return high, (x - high.astype(F32)).astype(BF16)


def dot(a, b):
    return jnp.dot(a, b, preferred_element_type=F32)


def params():
    return pltpu.CompilerParams(vmem_limit_bytes=VMEM_LIMIT)


def cost(flops, bytes_accessed):
    return pl.CostEstimate(flops=int(flops), bytes_accessed=int(bytes_accessed), transcendentals=0)


def in_vmem(x):
    return pltpu.with_memory_space_constraint(x, pltpu.VMEM)


def in_hbm(x):
    return pltpu.with_memory_space_constraint(x, pltpu.HBM)


def three(high, low, axis):
    return jnp.concatenate([high, high, low], axis=axis)


def three_other(high, low, axis):
    return jnp.concatenate([high, low, high], axis=axis)


def fetch_kernel(m_hbm, q_hbm, m_ref, high_ref, low_ref, q_ref, m_sem, q_sem):
    half = q_ref.shape[0] // 2
    spans = [pl.ds(k * half, half) for k in range(2)]
    copies = [pltpu.make_async_copy(q_hbm.at[span], q_ref.at[span], q_sem.at[k]) for k, span in enumerate(spans)]
    whole = pltpu.make_async_copy(m_hbm, m_ref, m_sem)
    for copy in copies:
        copy.start()
    whole.start()
    for copy, span in zip(copies, spans):
        copy.wait()
        high_ref[span, :], low_ref[span, :] = split(q_ref[span, :])
    whole.wait()


def fetch(momentum, factor):
    cols, rank = factor.shape
    return pl.pallas_call(
        fetch_kernel,
        in_specs=[HBM, HBM],
        out_specs=[ANY, VMEM, VMEM],
        out_shape=[
            pltpu.VMEM(momentum.shape, F32),
            pltpu.VMEM((cols, rank), BF16),
            pltpu.VMEM((cols, rank), BF16),
        ],
        scratch_shapes=[pltpu.VMEM((cols, rank), F32), pltpu.SemaphoreType.DMA, pltpu.SemaphoreType.DMA((2,))],
        compiler_params=params(),
        cost_estimate=cost(cols * rank, 4 * cols * (momentum.shape[0] + rank)),
        name="fetch",
    )(in_hbm(momentum), in_hbm(factor))


def left_kernel(at, m_ref, high_ref, low_ref, out_ref):
    half = high_ref.shape[0] // 2
    total = None
    for k in range(2):
        span = pl.ds(k * half, half)
        piece = m_ref[pl.ds(at, out_ref.shape[0]), span]
        part = dot(three(*split(piece), 1), three_other(high_ref[span, :], low_ref[span, :], 0))
        total = part if total is None else total + part
    out_ref[...] = total


def left_piece(momentum, high, low, at, size):
    cols, rank = high.shape
    return pl.pallas_call(
        lambda *refs: left_kernel(at, *refs),
        in_specs=[VMEM] * 3,
        out_specs=VMEM,
        out_shape=jax.ShapeDtypeStruct((size, rank), F32),
        compiler_params=params(),
        cost_estimate=cost(6 * size * cols * rank, 2**20),
        name="left",
    )(in_vmem(momentum), in_vmem(high), in_vmem(low))


def raw_kernel(at, groups, added, with_gram, order_ref, left_ref, m_ref, *refs):
    count = len(groups) + with_gram
    before_refs, out_refs = refs[: count * added], refs[count * added :]
    left = left_ref[...]
    lhs = three(*split(left.T), 1)
    if with_gram:
        gram = full_dot(left, left, ((0,), (0,)))
        out_refs[-1][...] = before_refs[-1][...] + gram if added else gram
    for g, places in enumerate(groups):
        width = out_refs[g].shape[2]
        for s, place in enumerate(places):
            span = pl.ds(pl.multiple_of(order_ref[place] * width, width), width)
            part = dot(lhs, three_other(*split(m_ref[pl.ds(at, left.shape[0]), span]), 0))
            out_refs[g][s] = before_refs[g][s] + part if added else part


def raw_pieces(order, groups, left, momentum, at, before, with_gram):
    rows, rank = left.shape
    width = momentum.shape[1] // RING
    chunks = sum(len(places) for places in groups)
    shapes = [jax.ShapeDtypeStruct((len(places), rank, width), F32) for places in groups]
    shapes += [jax.ShapeDtypeStruct((rank, rank), F32)] * with_gram
    return pl.pallas_call(
        lambda *refs: raw_kernel(at, groups, bool(before), with_gram, *refs),
        in_specs=[SMEM] + [VMEM] * (2 + len(before)),
        out_specs=[VMEM] * len(shapes),
        out_shape=shapes,
        compiler_params=params(),
        cost_estimate=cost(6 * rows * rank * width * chunks, 2**20),
        name="raw_right",
    )(order, left, in_vmem(momentum), *before)


def gram_kernel(chunks, order_ref, left_ref, before_ref, out_ref):
    left = left_ref[...]
    total = before_ref[...] + full_dot(left, left, ((0,), (0,)))
    half = total.shape[0] // 2
    first = order_ref[0] < chunks
    out_ref[0] = jnp.where(first, total[:half], total[half:])
    out_ref[1] = jnp.where(first, total[half:], total[:half])


def gram_halves(order, left, before):
    rank = left.shape[1]
    return pl.pallas_call(
        lambda *refs: gram_kernel(RING // 2, *refs),
        in_specs=[SMEM, VMEM, VMEM],
        out_specs=VMEM,
        out_shape=jax.ShapeDtypeStruct((2, rank // 2, rank), F32),
        compiler_params=params(),
        cost_estimate=cost(12 * rank * rank * left.shape[0], 2**20),
        name="gram",
    )(order, left, before)


def full_dot(a, b, contract=((1,), (0,))):
    return lax.dot_general(a, b, (contract, ((), ())), precision=HIGHEST, preferred_element_type=F32)


def rough_dot(a, b, contract=((1,), (0,))):
    return lax.dot_general(a.astype(BF16), b.astype(BF16), (contract, ((), ())), preferred_element_type=F32)


def split_dot(a, b, contract=((1,), (0,))):
    (a_high, a_low), (b_high, b_low) = split(a), split(b)
    return rough_dot(a_high, b_high, contract) + rough_dot(a_high, b_low, contract) + rough_dot(a_low, b_high, contract)


def newton(gram_ref, x_ref):
    rank = gram_ref.shape[0]
    rows = lax.broadcasted_iota(jnp.int32, (rank, rank), 0)
    cols = lax.broadcasted_iota(jnp.int32, (rank, rank), 1)
    eye = jnp.where(rows == cols, 1.0, 0.0).astype(F32)
    gram = gram_ref[...]
    x = eye * lax.rsqrt(jnp.sum(gram * eye, axis=1, keepdims=True))
    for times in (rough_dot, rough_dot, split_dot, full_dot):
        error = times(times(x, gram), x, ((1,), (1,))) - eye
        x = x - times(jnp.where(rows > cols, error, 0.5 * eye * error), x)
    x_ref[...] = x
    return jnp.sum(error * error), jnp.min(jnp.where(rows == cols, x, 1.0))


def eliminate(work_ref):
    rank = work_ref.shape[0]
    rows = lax.broadcasted_iota(jnp.int32, (rank, 2 * rank), 0)
    cols = lax.broadcasted_iota(jnp.int32, (rank, 2 * rank), 1)

    def step(j, carry):
        work = work_ref[...]
        row = work_ref[pl.ds(j, 1), :]
        pivot = jnp.sum(jnp.where(cols[:1] == j, row, 0.0), axis=1, keepdims=True)
        column = jnp.sum(jnp.where(cols == j, work, 0.0), axis=1, keepdims=True)
        ratio = jnp.where(rows[:, :1] > j, column * (1.0 / pivot), 0.0)
        work_ref[...] = work - ratio * row
        return carry

    lax.fori_loop(0, rank, step, 0)
    work = work_ref[...]
    pivots = jnp.sum(jnp.where(rows == cols, work, 0.0), axis=1, keepdims=True)
    return jnp.where(rows + rank >= cols, work / jnp.sqrt(pivots), 0.0)[:, rank:]


def factor_kernel(pieces, chunks, order_ref, kept_ref, sent_ref, *refs):
    left_refs = refs[:pieces]
    inv_ref, orth_ref, operand_ref, gram_ref, work_ref = refs[pieces:]
    half, rank = kept_ref.shape
    first = order_ref[0] < chunks
    gram_ref[:half] = jnp.where(first, kept_ref[...], sent_ref[...])
    gram_ref[half:] = jnp.where(first, sent_ref[...], kept_ref[...])
    before, least = newton(gram_ref, inv_ref)

    @pl.when(jnp.logical_not((before < 1e-6) & (least > 0.0)))
    def _():
        rows = lax.broadcasted_iota(jnp.int32, (rank, rank), 0)
        cols = lax.broadcasted_iota(jnp.int32, (rank, rank), 1)
        work_ref[:, :rank] = gram_ref[...]
        work_ref[:, rank:] = jnp.where(rows == cols, 1.0, 0.0).astype(F32)
        inv_ref[...] = eliminate(work_ref)

    inverse = three_other(*split(inv_ref[...]), 1)
    at = 0
    for ref in left_refs:
        size = ref.shape[0]
        orth = lax.dot_general(
            three(*split(ref[...]), 1), inverse, (((1,), (1,)), ((), ())), preferred_element_type=F32
        )
        orth_ref[at : at + size, :] = orth
        operand_ref[at : at + size, :] = three(*split(-0.5 * orth), 1)
        at += size


def factor(order, kept, sent, lefts):
    rank = kept.shape[1]
    rows = sum(x.shape[0] for x in lefts)
    return pl.pallas_call(
        lambda *refs: factor_kernel(len(lefts), RING // 2, *refs),
        in_specs=[SMEM] + [VMEM] * (2 + len(lefts)),
        out_specs=[VMEM] * 3,
        out_shape=[
            jax.ShapeDtypeStruct((rank, rank), F32),
            jax.ShapeDtypeStruct((rows, rank), F32),
            jax.ShapeDtypeStruct((rows, 3 * rank), BF16),
        ],
        scratch_shapes=[pltpu.VMEM((rank, rank), F32), pltpu.VMEM((rank, 2 * rank), F32)],
        compiler_params=params(),
        cost_estimate=cost(1, 1),
        name="factor",
    )(order, kept, sent, *lefts)


def square_kernel(inv_ref, raw_ref, out_ref):
    right = jnp.dot(inv_ref[...], raw_ref[0], precision=HIGHEST, preferred_element_type=F32)
    ones = jnp.ones((8, right.shape[1]), F32)
    out_ref[...] = lax.dot_general(
        ones, right * right, (((1,), (1,)), ((), ())), precision=HIGHEST, preferred_element_type=F32
    )


def square_row(inverse, raw):
    rank = inverse.shape[0]
    return pl.pallas_call(
        square_kernel,
        out_shape=jax.ShapeDtypeStruct((8, rank), F32),
        compiler_params=params(),
        cost_estimate=cost(12 * rank * rank * raw.shape[2], 2**20),
        name="squares",
    )(inverse, raw)


def operand_kernel(count, scale, *refs):
    square_refs = refs[:count]
    orth_ref, operand_ref = refs[count:]
    squares = square_refs[0][...]
    for ref in square_refs[1:]:
        squares = squares + ref[...]
    norm = scale / jnp.sqrt(squares[:1] + 1e-06)
    operand_ref[...] = three(*split(orth_ref[...] * norm), 1)


def update_operand(squares, orth, scale):
    rows, rank = orth.shape
    return pl.pallas_call(
        lambda *refs: operand_kernel(len(squares), scale, *refs),
        out_shape=jax.ShapeDtypeStruct((rows, 3 * rank), BF16),
        compiler_params=params(),
        cost_estimate=cost(rows * rank * 10, rows * rank * 12),
        name="operand",
    )(*squares, orth)


def new_kernel(places, chained, order_ref, operand_ref, inv_ref, m_ref, *refs):
    count = len(places)
    raw_refs, refs = refs[:count], refs[count + chained :]
    out_hbm, right_refs, (out_ref, sem) = refs[0], refs[1 : 1 + count], refs[1 + count :]
    _, rows, width = out_ref.shape
    parts = sem.shape[1]
    tile = rows // parts
    inverse = three(*split(inv_ref[...]), 1)
    for raw_ref, right_ref in zip(raw_refs, right_refs):
        right = dot(inverse, three_other(*split(raw_ref[0]), 0))
        right_ref[...] = three_other(*split(right), 0)
    copies = []
    for s, right_ref in enumerate(right_refs):
        span = pl.ds(pl.multiple_of(order_ref[places[s]] * width, width), width)
        right = right_ref[...]
        for part in range(parts):
            at = pl.ds(part * tile, tile)
            out_ref[s, at] = m_ref[at, span] + dot(operand_ref[at, :], right)
            copies.append(pltpu.make_async_copy(out_ref.at[s, at], out_hbm.at[at, span], sem.at[s, part]))
            copies[-1].start()
    for copy in copies:
        copy.wait()


def new_chunks(order, places, operand, inverse, raws, momentum, before):
    rows, cols = momentum.shape
    _, rank, width = raws[0].shape
    count, parts = len(raws), 4
    outs = pl.pallas_call(
        lambda *refs: new_kernel(places, len(before), *refs),
        in_specs=[SMEM] + [VMEM] * (3 + count) + [HBM] * len(before),
        out_specs=[HBM] + [VMEM] * count,
        out_shape=[jax.ShapeDtypeStruct((rows, cols), F32)]
        + [jax.ShapeDtypeStruct((3 * rank, width), BF16)] * count,
        scratch_shapes=[pltpu.VMEM((count, rows, width), F32), pltpu.SemaphoreType.DMA((count, parts))],
        input_output_aliases={4 + count: 0} if before else {},
        compiler_params=params(),
        cost_estimate=cost(6 * count * rows * rank * width, 4 * count * rows * width),
        name="new_momentum",
    )(order, operand, inverse, in_vmem(momentum), *raws, *before)
    return [outs[0]], list(outs[1:])


def finish_kernel(places, done, order_ref, operand_ref, scaled_ref, inv_ref, m_ref, *refs):
    count = len(places)
    raw_refs, right_refs, refs = refs[:count], refs[count : count + len(done)], refs[count + len(done) + 1 :]
    new_hbm, update_hbm, right_ref, out_ref, sem = refs
    buffers, rows, width = out_ref.shape
    parts = sem.shape[1]
    tile = rows // parts
    inverse = three(*split(inv_ref[...]), 1)
    copies = []

    def store(place, lhs_ref, ref, out_hbm, added):
        slot = len(copies) % buffers
        if len(copies) >= buffers:
            for copy in copies[-buffers]:
                copy.wait()
        span = pl.ds(pl.multiple_of(order_ref[place] * width, width), width)
        right = ref[...]
        copies.append([])
        for part in range(parts):
            at = pl.ds(part * tile, tile)
            total = dot(lhs_ref[at, :], right)
            out_ref[slot, at] = m_ref[at, span] + total if added else total
            copies[-1].append(pltpu.make_async_copy(out_ref.at[slot, at], out_hbm.at[at, span], sem.at[slot, part]))
            copies[-1][-1].start()

    for n, place in enumerate(places):
        right = dot(inverse, three_other(*split(raw_refs[n][0]), 0))
        right_ref[n % 2] = three_other(*split(right), 0)
        store(place, operand_ref, right_ref.at[n % 2], new_hbm, True)
        store(place, scaled_ref, right_ref.at[n % 2], update_hbm, False)
        if n < len(done):
            store(done[n], scaled_ref, right_refs[n], update_hbm, False)
    for job in copies[-buffers:]:
        for copy in job:
            copy.wait()


def finish(order, places, done, operand, scaled, inverse, momentum, raws, rights, new):
    rows, cols = momentum.shape
    _, rank, width = raws[0].shape
    count, parts, buffers = len(raws), 4, 6
    whole = jax.ShapeDtypeStruct((rows, cols), F32)
    return pl.pallas_call(
        lambda *refs: finish_kernel(places, done, *refs),
        in_specs=[SMEM] + [VMEM] * (4 + count + len(rights)) + [HBM],
        out_specs=[HBM, HBM],
        out_shape=[whole, whole],
        scratch_shapes=[
            pltpu.VMEM((2, 3 * rank, width), BF16),
            pltpu.VMEM((buffers, rows, width), F32),
            pltpu.SemaphoreType.DMA((buffers, parts)),
        ],
        input_output_aliases={5 + count + len(rights): 0},
        compiler_params=params(),
        cost_estimate=cost(6 * 3 * count * rows * rank * width, 4 * 3 * count * rows * width),
        name="finish",
    )(order, operand, scaled, inverse, in_vmem(momentum), *raws, *rights, new)


def add_kernel(*refs):
    refs[-1][...] = sum((ref[...] for ref in refs[1:-1]), refs[0][...])


def add(*values):
    return pl.pallas_call(
        add_kernel,
        in_specs=[VMEM] * len(values),
        out_specs=VMEM,
        out_shape=jax.ShapeDtypeStruct(values[0].shape, F32),
        compiler_params=params(),
        cost_estimate=cost(values[0].size, 1),
        name="add",
    )(*values)


def half_kernel(*refs):
    *value_refs, second_ref, first_ref = refs
    half = first_ref.shape[0]
    second_ref[...] = sum((ref[half:] for ref in value_refs[1:]), value_refs[0][half:])
    first_ref[...] = sum((ref[:half] for ref in value_refs[1:]), value_refs[0][:half])


def add_halves(*values):
    half = values[0].shape[0] // 2
    shape = jax.ShapeDtypeStruct((half, *values[0].shape[1:]), F32)
    return pl.pallas_call(
        half_kernel,
        in_specs=[VMEM] * len(values),
        out_specs=[VMEM] * 2,
        out_shape=[shape] * 2,
        compiler_params=params(),
        cost_estimate=cost(values[0].size, 1),
        name="add_halves",
    )(*values)


def choose_kernel(order_ref, a_ref, b_ref, out_ref):
    out_ref[...] = jnp.where(order_ref[RING] > 0, a_ref[...], b_ref[...])


def choose(order, a, b):
    return pl.pallas_call(
        choose_kernel,
        in_specs=[SMEM, VMEM, VMEM],
        out_specs=VMEM,
        out_shape=jax.ShapeDtypeStruct(a.shape, F32),
        compiler_params=params(),
        cost_estimate=cost(a.size, 1),
        name="choose",
    )(order, a, b)


PAIR = [(r, r ^ 1) for r in range(RING)]
NEAR = [(r, r ^ (2 if r % 2 == 0 else 4)) for r in range(RING)]
FAR = [(r, r ^ (4 if r % 2 == 0 else 2)) for r in range(RING)]
ACROSS = [(r, r ^ 6) for r in range(RING)]


def along(x, pairs):
    return lax.ppermute(x, "row", pairs)


def together(*values):
    return lax.optimization_barrier(values)


def local(momentum, right_factor, scale):
    rows, cols = momentum.shape
    me, at = lax.axis_index("row"), lax.axis_index("col")
    core, first, second = me % 2, me // 2 % 2, me // 4
    low_id = jnp.where(core == 0, 2 * first + second, 2 * second + first)
    pair_id = jnp.where(core == 0, 2 * second + first, 2 * first + second)
    slots = jnp.arange(RING + 1, dtype=jnp.int32)
    order = jnp.where(slots < 4, 4 * core + (slots ^ low_id), 4 * (1 - core) + ((slots - 4) ^ pair_id))
    order = jnp.where(slots < RING, order, (at > 0) & (at < LINE - 1)).astype(jnp.int32)
    order, right_factor = together(order, right_factor)

    resident, high, low = fetch(momentum, right_factor)
    sizes = [rows // 8 * share for share in SHARES]
    starts = [sum(sizes[:k]) for k in range(len(sizes))]

    def left_of(k, high):
        return left_piece(resident, high, low, starts[k], sizes[k])

    def inward(x):
        return lax.ppermute(x, "col", [(0, 1), (3, 2)])

    def across(x):
        return lax.ppermute(x, "col", [(1, 2), (2, 1)])

    def outward(x):
        return lax.ppermute(x, "col", [(1, 0), (2, 3)])

    *early, final = range(len(sizes))
    parts = [left_of(k, high) for k in early]
    held = [add(part, inward(part)) for part in parts]
    high, held[0] = together(high, held[0])
    part = left_of(final, high)
    held.append(add(part, inward(part)))
    crossed = [add(x, across(x)) for x in held[:-1]]
    held[-1], crossed[0] = together(held[-1], crossed[0])
    crossed.append(add(held[-1], across(held[-1])))
    lefts = [choose(order, x, outward(x)) for x in crossed]

    groups = ((7, 6), (3, 2), (5, 4), (1, 0))
    sums = []
    for k in early:
        sums = raw_pieces(order, groups, lefts[k], resident, starts[k], sums, 1)
    *sums, gram = sums

    def last(order, g):
        return raw_pieces(order, groups[g : g + 1], lefts[-1], resident, starts[-1], [sums[g]], 0)[0]

    sent_far = last(order, 0)
    order_1, sent_far = together(order, sent_far)
    halves = gram_halves(order_1, lefts[-1], gram)
    order_2, halves = together(order_1, halves)
    kept_far = last(order_2, 1)
    kept_far = add(kept_far, along(sent_far, PAIR))
    got_near = along(kept_far, NEAR)
    kept = add(halves[0], along(halves[1], PAIR))
    order_3, kept_far, kept = together(order_2, kept_far, kept)
    sent_near, kept_near = last(order_3, 2), last(order_3, 3)
    kept = add(kept, *[along(kept, pairs) for pairs in (NEAR, FAR, ACROSS)])
    got_near, kept = together(got_near, kept)
    slot_0, slot_1 = add_halves(kept_near, along(sent_near, PAIR), got_near)
    got_own = along(slot_1, FAR)
    inverse, orth, operand = factor(order, kept, along(kept, PAIR), lefts)
    got_own, inverse = together(got_own, inverse)
    own = add(slot_0, got_own)

    def new_pair(slot, raws, before):
        return new_chunks(order, (slot, slot + 4), operand, inverse, raws, resident, before)

    chunk_1, pair = along(own, FAR), along(own, PAIR)
    squares = square_row(inverse, own)
    squares = add(squares, along(squares, PAIR))
    squares, again = together(squares, own)
    got, chunk_2 = along(squares, NEAR), along(again, NEAR)
    new, rights = new_chunks(order, (0, 4), operand, inverse, [own, pair], resident, [])
    got, chunk_1, new[0] = together(got, chunk_1, new[0])
    chunk_3, pair_1 = along(chunk_1, NEAR), along(chunk_1, PAIR)
    squares = add(squares, got)
    got = along(squares, FAR)
    pair_1, chunk_2 = together(pair_1, chunk_2)
    new, right = new_chunks(order, (1, 5), operand, inverse, [chunk_1, pair_1], resident, new)
    rights += right
    got, chunk_2, chunk_3, new[0] = together(got, chunk_2, chunk_3, new[0])
    pair_2, pair_3 = along(chunk_2, PAIR), along(chunk_3, PAIR)
    squares = add(squares, got)
    gots = [lax.ppermute(squares, "col", [(c, c ^ d) for c in range(LINE)]) for d in range(1, LINE)]
    scaled = update_operand([squares] + gots, orth, scale)
    raws = [chunk_2, pair_2, chunk_3, pair_3]
    return tuple(
        finish(order, (2, 6, 3, 7), (0, 4, 1, 5), operand, scaled, inverse, resident, raws, rights, new[0])
    )


def general(momentum, right_factor, scale):
    left = lax.psum(jnp.dot(momentum, right_factor, precision=HIGHEST), "col")
    gram_part = jnp.dot(left.T, left, precision=HIGHEST)
    raw_part = jnp.dot(left.T, momentum, precision=HIGHEST)
    gram, raw = lax.psum((gram_part, raw_part), "row")
    lower = jnp.linalg.cholesky(gram)
    orth = jax.scipy.linalg.solve_triangular(lower, left.T, lower=True).T
    right = jax.scipy.linalg.solve_triangular(lower, raw, lower=True)
    squares = lax.psum(jnp.sum(right * right, axis=1, keepdims=True), "col")
    factor_q = right / jnp.sqrt(squares + 1e-06)
    new = momentum - 0.5 * jnp.dot(orth, right, precision=HIGHEST)
    return new, scale * jnp.dot(orth, factor_q, precision=HIGHEST)


def solution(mesh):
    by_hand = mesh.shape["row"] == RING and mesh.shape["col"] == LINE
    program = local if by_hand else general

    def run(momentum, right_factor):
        rows, cols = momentum.shape
        scale = math.sqrt(rows * cols / right_factor.shape[1])
        return jax.shard_map(
            lambda m, q: program(m, q, scale),
            mesh=mesh,
            in_specs=(P("row", "col"), P("col", None)),
            out_specs=(P("row", "col"), P("row", "col")),
            check_vma=False,
        )(momentum, right_factor)

    return run
```

```python
import math

import jax
import jax.numpy as jnp
from jax import lax
from jax.experimental import pallas as pl
from jax.experimental.pallas import tpu as pltpu
from jax.sharding import PartitionSpec as P

F32 = jnp.float32
BF16 = jnp.bfloat16
HIGHEST = lax.Precision.HIGHEST
VMEM_LIMIT = 20 * 1024 * 1024
SMEM = pl.BlockSpec(memory_space=pltpu.SMEM)
VMEM = pl.BlockSpec(memory_space=pltpu.VMEM)
HBM = pl.BlockSpec(memory_space=pltpu.HBM)
ANY = pl.BlockSpec(memory_space=pl.ANY)
LINE = 4
RING = 8
SHARES = (3, 3, 2)


def split(x):
    high = x.astype(BF16)
    return high, (x - high.astype(F32)).astype(BF16)


def dot(a, b):
    return jnp.dot(a, b, preferred_element_type=F32)


def params():
    return pltpu.CompilerParams(vmem_limit_bytes=VMEM_LIMIT)


def cost(flops, bytes_accessed):
    return pl.CostEstimate(flops=int(flops), bytes_accessed=int(bytes_accessed), transcendentals=0)


def in_vmem(x):
    return pltpu.with_memory_space_constraint(x, pltpu.VMEM)


def in_hbm(x):
    return pltpu.with_memory_space_constraint(x, pltpu.HBM)


def three(high, low, axis):
    return jnp.concatenate([high, high, low], axis=axis)


def three_other(high, low, axis):
    return jnp.concatenate([high, low, high], axis=axis)


def fetch_kernel(m_hbm, q_hbm, m_ref, high_ref, low_ref, q_ref, m_sem, q_sem):
    half = q_ref.shape[0] // 2
    spans = [pl.ds(k * half, half) for k in range(2)]
    copies = [pltpu.make_async_copy(q_hbm.at[span], q_ref.at[span], q_sem.at[k]) for k, span in enumerate(spans)]
    whole = pltpu.make_async_copy(m_hbm, m_ref, m_sem)
    for copy in copies:
        copy.start()
    whole.start()
    for copy, span in zip(copies, spans):
        copy.wait()
        high_ref[span, :], low_ref[span, :] = split(q_ref[span, :])
    whole.wait()


def fetch(momentum, factor):
    cols, rank = factor.shape
    return pl.pallas_call(
        fetch_kernel,
        in_specs=[HBM, HBM],
        out_specs=[ANY, VMEM, VMEM],
        out_shape=[
            pltpu.VMEM(momentum.shape, F32),
            pltpu.VMEM((cols, rank), BF16),
            pltpu.VMEM((cols, rank), BF16),
        ],
        scratch_shapes=[pltpu.VMEM((cols, rank), F32), pltpu.SemaphoreType.DMA, pltpu.SemaphoreType.DMA((2,))],
        compiler_params=params(),
        cost_estimate=cost(cols * rank, 4 * cols * (momentum.shape[0] + rank)),
        name="fetch",
    )(in_hbm(momentum), in_hbm(factor))


def left_kernel(at, m_ref, high_ref, low_ref, out_ref):
    half = high_ref.shape[0] // 2
    total = None
    for k in range(2):
        span = pl.ds(k * half, half)
        piece = m_ref[pl.ds(at, out_ref.shape[0]), span]
        part = dot(three(*split(piece), 1), three_other(high_ref[span, :], low_ref[span, :], 0))
        total = part if total is None else total + part
    out_ref[...] = total


def left_piece(momentum, high, low, at, size):
    cols, rank = high.shape
    return pl.pallas_call(
        lambda *refs: left_kernel(at, *refs),
        in_specs=[VMEM] * 3,
        out_specs=VMEM,
        out_shape=jax.ShapeDtypeStruct((size, rank), F32),
        compiler_params=params(),
        cost_estimate=cost(6 * size * cols * rank, 2**20),
        name="left",
    )(in_vmem(momentum), in_vmem(high), in_vmem(low))


def raw_kernel(at, groups, added, with_gram, order_ref, left_ref, m_ref, *refs):
    count = len(groups) + with_gram
    before_refs, out_refs = refs[: count * added], refs[count * added :]
    left = left_ref[...]
    lhs = three(*split(left.T), 1)
    if with_gram:
        gram = full_dot(left, left, ((0,), (0,)))
        out_refs[-1][...] = before_refs[-1][...] + gram if added else gram
    for g, places in enumerate(groups):
        width = out_refs[g].shape[2]
        for s, place in enumerate(places):
            span = pl.ds(pl.multiple_of(order_ref[place] * width, width), width)
            part = dot(lhs, three_other(*split(m_ref[pl.ds(at, left.shape[0]), span]), 0))
            out_refs[g][s] = before_refs[g][s] + part if added else part


def raw_pieces(order, groups, left, momentum, at, before, with_gram):
    rows, rank = left.shape
    width = momentum.shape[1] // RING
    chunks = sum(len(places) for places in groups)
    shapes = [jax.ShapeDtypeStruct((len(places), rank, width), F32) for places in groups]
    shapes += [jax.ShapeDtypeStruct((rank, rank), F32)] * with_gram
    return pl.pallas_call(
        lambda *refs: raw_kernel(at, groups, bool(before), with_gram, *refs),
        in_specs=[SMEM] + [VMEM] * (2 + len(before)),
        out_specs=[VMEM] * len(shapes),
        out_shape=shapes,
        compiler_params=params(),
        cost_estimate=cost(6 * rows * rank * width * chunks, 2**20),
        name="raw_right",
    )(order, left, in_vmem(momentum), *before)


def gram_kernel(chunks, order_ref, left_ref, before_ref, out_ref):
    left = left_ref[...]
    total = before_ref[...] + full_dot(left, left, ((0,), (0,)))
    half = total.shape[0] // 2
    first = order_ref[0] < chunks
    out_ref[0] = jnp.where(first, total[:half], total[half:])
    out_ref[1] = jnp.where(first, total[half:], total[:half])


def gram_halves(order, left, before):
    rank = left.shape[1]
    return pl.pallas_call(
        lambda *refs: gram_kernel(RING // 2, *refs),
        in_specs=[SMEM, VMEM, VMEM],
        out_specs=VMEM,
        out_shape=jax.ShapeDtypeStruct((2, rank // 2, rank), F32),
        compiler_params=params(),
        cost_estimate=cost(12 * rank * rank * left.shape[0], 2**20),
        name="gram",
    )(order, left, before)


def full_dot(a, b, contract=((1,), (0,))):
    return lax.dot_general(a, b, (contract, ((), ())), precision=HIGHEST, preferred_element_type=F32)


def rough_dot(a, b, contract=((1,), (0,))):
    return lax.dot_general(a.astype(BF16), b.astype(BF16), (contract, ((), ())), preferred_element_type=F32)


def split_dot(a, b, contract=((1,), (0,))):
    (a_high, a_low), (b_high, b_low) = split(a), split(b)
    return rough_dot(a_high, b_high, contract) + rough_dot(a_high, b_low, contract) + rough_dot(a_low, b_high, contract)


def newton(gram_ref, x_ref):
    rank = gram_ref.shape[0]
    rows = lax.broadcasted_iota(jnp.int32, (rank, rank), 0)
    cols = lax.broadcasted_iota(jnp.int32, (rank, rank), 1)
    eye = jnp.where(rows == cols, 1.0, 0.0).astype(F32)
    gram = gram_ref[...]
    x = eye * lax.rsqrt(jnp.sum(gram * eye, axis=1, keepdims=True))
    for times in (rough_dot, rough_dot, split_dot, full_dot):
        error = times(times(x, gram), x, ((1,), (1,))) - eye
        x = x - times(jnp.where(rows > cols, error, 0.5 * eye * error), x)
    x_ref[...] = x
    return jnp.sum(error * error), jnp.min(jnp.where(rows == cols, x, 1.0))


def eliminate(work_ref):
    rank = work_ref.shape[0]
    rows = lax.broadcasted_iota(jnp.int32, (rank, 2 * rank), 0)
    cols = lax.broadcasted_iota(jnp.int32, (rank, 2 * rank), 1)

    def step(j, carry):
        work = work_ref[...]
        row = work_ref[pl.ds(j, 1), :]
        pivot = jnp.sum(jnp.where(cols[:1] == j, row, 0.0), axis=1, keepdims=True)
        column = jnp.sum(jnp.where(cols == j, work, 0.0), axis=1, keepdims=True)
        ratio = jnp.where(rows[:, :1] > j, column * (1.0 / pivot), 0.0)
        work_ref[...] = work - ratio * row
        return carry

    lax.fori_loop(0, rank, step, 0)
    work = work_ref[...]
    pivots = jnp.sum(jnp.where(rows == cols, work, 0.0), axis=1, keepdims=True)
    return jnp.where(rows + rank >= cols, work / jnp.sqrt(pivots), 0.0)[:, rank:]


def factor_kernel(pieces, chunks, order_ref, kept_ref, sent_ref, *refs):
    left_refs = refs[:pieces]
    inv_ref, orth_ref, operand_ref, gram_ref, work_ref = refs[pieces:]
    half, rank = kept_ref.shape
    first = order_ref[0] < chunks
    gram_ref[:half] = jnp.where(first, kept_ref[...], sent_ref[...])
    gram_ref[half:] = jnp.where(first, sent_ref[...], kept_ref[...])
    before, least = newton(gram_ref, inv_ref)

    @pl.when(jnp.logical_not((before < 1e-6) & (least > 0.0)))
    def _():
        rows = lax.broadcasted_iota(jnp.int32, (rank, rank), 0)
        cols = lax.broadcasted_iota(jnp.int32, (rank, rank), 1)
        work_ref[:, :rank] = gram_ref[...]
        work_ref[:, rank:] = jnp.where(rows == cols, 1.0, 0.0).astype(F32)
        inv_ref[...] = eliminate(work_ref)

    inverse = three_other(*split(inv_ref[...]), 1)
    at = 0
    for ref in left_refs:
        size = ref.shape[0]
        orth = lax.dot_general(
            three(*split(ref[...]), 1), inverse, (((1,), (1,)), ((), ())), preferred_element_type=F32
        )
        orth_ref[at : at + size, :] = orth
        operand_ref[at : at + size, :] = three(*split(-0.5 * orth), 1)
        at += size


def factor(order, kept, sent, lefts):
    rank = kept.shape[1]
    rows = sum(x.shape[0] for x in lefts)
    return pl.pallas_call(
        lambda *refs: factor_kernel(len(lefts), RING // 2, *refs),
        in_specs=[SMEM] + [VMEM] * (2 + len(lefts)),
        out_specs=[VMEM] * 3,
        out_shape=[
            jax.ShapeDtypeStruct((rank, rank), F32),
            jax.ShapeDtypeStruct((rows, rank), F32),
            jax.ShapeDtypeStruct((rows, 3 * rank), BF16),
        ],
        scratch_shapes=[pltpu.VMEM((rank, rank), F32), pltpu.VMEM((rank, 2 * rank), F32)],
        compiler_params=params(),
        cost_estimate=cost(1, 1),
        name="factor",
    )(order, kept, sent, *lefts)


def square_kernel(inv_ref, raw_ref, out_ref):
    right = jnp.dot(inv_ref[...], raw_ref[0], precision=HIGHEST, preferred_element_type=F32)
    ones = jnp.ones((8, right.shape[1]), F32)
    out_ref[...] = lax.dot_general(
        ones, right * right, (((1,), (1,)), ((), ())), precision=HIGHEST, preferred_element_type=F32
    )


def square_row(inverse, raw):
    rank = inverse.shape[0]
    return pl.pallas_call(
        square_kernel,
        out_shape=jax.ShapeDtypeStruct((8, rank), F32),
        compiler_params=params(),
        cost_estimate=cost(12 * rank * rank * raw.shape[2], 2**20),
        name="squares",
    )(inverse, raw)


def operand_kernel(count, scale, *refs):
    square_refs = refs[:count]
    orth_ref, operand_ref = refs[count:]
    squares = square_refs[0][...]
    for ref in square_refs[1:]:
        squares = squares + ref[...]
    norm = scale / jnp.sqrt(squares[:1] + 1e-06)
    operand_ref[...] = three(*split(orth_ref[...] * norm), 1)


def update_operand(squares, orth, scale):
    rows, rank = orth.shape
    return pl.pallas_call(
        lambda *refs: operand_kernel(len(squares), scale, *refs),
        out_shape=jax.ShapeDtypeStruct((rows, 3 * rank), BF16),
        compiler_params=params(),
        cost_estimate=cost(rows * rank * 10, rows * rank * 12),
        name="operand",
    )(*squares, orth)


def new_kernel(places, chained, order_ref, operand_ref, inv_ref, m_ref, *refs):
    count = len(places)
    raw_refs, refs = refs[:count], refs[count + chained :]
    out_hbm, right_refs, (out_ref, sem) = refs[0], refs[1 : 1 + count], refs[1 + count :]
    _, rows, width = out_ref.shape
    parts = sem.shape[1]
    tile = rows // parts
    inverse = three(*split(inv_ref[...]), 1)
    for raw_ref, right_ref in zip(raw_refs, right_refs):
        right = dot(inverse, three_other(*split(raw_ref[0]), 0))
        right_ref[...] = three_other(*split(right), 0)
    copies = []
    for s, right_ref in enumerate(right_refs):
        span = pl.ds(pl.multiple_of(order_ref[places[s]] * width, width), width)
        right = right_ref[...]
        for part in range(parts):
            at = pl.ds(part * tile, tile)
            out_ref[s, at] = m_ref[at, span] + dot(operand_ref[at, :], right)
            copies.append(pltpu.make_async_copy(out_ref.at[s, at], out_hbm.at[at, span], sem.at[s, part]))
            copies[-1].start()
    for copy in copies:
        copy.wait()


def new_chunks(order, places, operand, inverse, raws, momentum, before):
    rows, cols = momentum.shape
    _, rank, width = raws[0].shape
    count, parts = len(raws), 4
    outs = pl.pallas_call(
        lambda *refs: new_kernel(places, len(before), *refs),
        in_specs=[SMEM] + [VMEM] * (3 + count) + [HBM] * len(before),
        out_specs=[HBM] + [VMEM] * count,
        out_shape=[jax.ShapeDtypeStruct((rows, cols), F32)]
        + [jax.ShapeDtypeStruct((3 * rank, width), BF16)] * count,
        scratch_shapes=[pltpu.VMEM((count, rows, width), F32), pltpu.SemaphoreType.DMA((count, parts))],
        input_output_aliases={4 + count: 0} if before else {},
        compiler_params=params(),
        cost_estimate=cost(6 * count * rows * rank * width, 4 * count * rows * width),
        name="new_momentum",
    )(order, operand, inverse, in_vmem(momentum), *raws, *before)
    return [outs[0]], list(outs[1:])


def finish_kernel(places, done, order_ref, operand_ref, scaled_ref, inv_ref, m_ref, *refs):
    count = len(places)
    raw_refs, right_refs, refs = refs[:count], refs[count : count + len(done)], refs[count + len(done) + 1 :]
    new_hbm, update_hbm, right_ref, out_ref, sem = refs
    buffers, rows, width = out_ref.shape
    parts = sem.shape[1]
    tile = rows // parts
    inverse = three(*split(inv_ref[...]), 1)
    copies = []

    def store(place, lhs_ref, ref, out_hbm, added):
        slot = len(copies) % buffers
        if len(copies) >= buffers:
            for copy in copies[-buffers]:
                copy.wait()
        span = pl.ds(pl.multiple_of(order_ref[place] * width, width), width)
        right = ref[...]
        copies.append([])
        for part in range(parts):
            at = pl.ds(part * tile, tile)
            total = dot(lhs_ref[at, :], right)
            out_ref[slot, at] = m_ref[at, span] + total if added else total
            copies[-1].append(pltpu.make_async_copy(out_ref.at[slot, at], out_hbm.at[at, span], sem.at[slot, part]))
            copies[-1][-1].start()

    for n, place in enumerate(places):
        right = dot(inverse, three_other(*split(raw_refs[n][0]), 0))
        right_ref[n % 2] = three_other(*split(right), 0)
        store(place, operand_ref, right_ref.at[n % 2], new_hbm, True)
        store(place, scaled_ref, right_ref.at[n % 2], update_hbm, False)
        if n < len(done):
            store(done[n], scaled_ref, right_refs[n], update_hbm, False)
    for job in copies[-buffers:]:
        for copy in job:
            copy.wait()


def finish(order, places, done, operand, scaled, inverse, momentum, raws, rights, new):
    rows, cols = momentum.shape
    _, rank, width = raws[0].shape
    count, parts, buffers = len(raws), 4, 6
    whole = jax.ShapeDtypeStruct((rows, cols), F32)
    return pl.pallas_call(
        lambda *refs: finish_kernel(places, done, *refs),
        in_specs=[SMEM] + [VMEM] * (4 + count + len(rights)) + [HBM],
        out_specs=[HBM, HBM],
        out_shape=[whole, whole],
        scratch_shapes=[
            pltpu.VMEM((2, 3 * rank, width), BF16),
            pltpu.VMEM((buffers, rows, width), F32),
            pltpu.SemaphoreType.DMA((buffers, parts)),
        ],
        input_output_aliases={5 + count + len(rights): 0},
        compiler_params=params(),
        cost_estimate=cost(6 * 3 * count * rows * rank * width, 4 * 3 * count * rows * width),
        name="finish",
    )(order, operand, scaled, inverse, in_vmem(momentum), *raws, *rights, new)


def add_kernel(*refs):
    refs[-1][...] = sum((ref[...] for ref in refs[1:-1]), refs[0][...])


def add(*values):
    return pl.pallas_call(
        add_kernel,
        in_specs=[VMEM] * len(values),
        out_specs=VMEM,
        out_shape=jax.ShapeDtypeStruct(values[0].shape, F32),
        compiler_params=params(),
        cost_estimate=cost(values[0].size, 1),
        name="add",
    )(*values)


def half_kernel(*refs):
    *value_refs, second_ref, first_ref = refs
    half = first_ref.shape[0]
    second_ref[...] = sum((ref[half:] for ref in value_refs[1:]), value_refs[0][half:])
    first_ref[...] = sum((ref[:half] for ref in value_refs[1:]), value_refs[0][:half])


def add_halves(*values):
    half = values[0].shape[0] // 2
    shape = jax.ShapeDtypeStruct((half, *values[0].shape[1:]), F32)
    return pl.pallas_call(
        half_kernel,
        in_specs=[VMEM] * len(values),
        out_specs=[VMEM] * 2,
        out_shape=[shape] * 2,
        compiler_params=params(),
        cost_estimate=cost(values[0].size, 1),
        name="add_halves",
    )(*values)


def choose_kernel(order_ref, a_ref, b_ref, out_ref):
    out_ref[...] = jnp.where(order_ref[RING] > 0, a_ref[...], b_ref[...])


def choose(order, a, b):
    return pl.pallas_call(
        choose_kernel,
        in_specs=[SMEM, VMEM, VMEM],
        out_specs=VMEM,
        out_shape=jax.ShapeDtypeStruct(a.shape, F32),
        compiler_params=params(),
        cost_estimate=cost(a.size, 1),
        name="choose",
    )(order, a, b)


PAIR = [(r, r ^ 1) for r in range(RING)]
NEAR = [(r, r ^ (2 if r % 2 == 0 else 4)) for r in range(RING)]
FAR = [(r, r ^ (4 if r % 2 == 0 else 2)) for r in range(RING)]
ACROSS = [(r, r ^ 6) for r in range(RING)]


def along(x, pairs):
    return lax.ppermute(x, "row", pairs)


def together(*values):
    return lax.optimization_barrier(values)


def local(momentum, right_factor, scale):
    rows, cols = momentum.shape
    me, at = lax.axis_index("row"), lax.axis_index("col")
    core, first, second = me % 2, me // 2 % 2, me // 4
    low_id = jnp.where(core == 0, 2 * first + second, 2 * second + first)
    pair_id = jnp.where(core == 0, 2 * second + first, 2 * first + second)
    slots = jnp.arange(RING + 1, dtype=jnp.int32)
    order = jnp.where(slots < 4, 4 * core + (slots ^ low_id), 4 * (1 - core) + ((slots - 4) ^ pair_id))
    order = jnp.where(slots < RING, order, (at > 0) & (at < LINE - 1)).astype(jnp.int32)
    order, right_factor = together(order, right_factor)

    resident, high, low = fetch(momentum, right_factor)
    sizes = [rows // 8 * share for share in SHARES]
    starts = [sum(sizes[:k]) for k in range(len(sizes))]

    def left_of(k, high):
        return left_piece(resident, high, low, starts[k], sizes[k])

    def inward(x):
        return lax.ppermute(x, "col", [(0, 1), (3, 2)])

    def across(x):
        return lax.ppermute(x, "col", [(1, 2), (2, 1)])

    def outward(x):
        return lax.ppermute(x, "col", [(1, 0), (2, 3)])

    *early, final = range(len(sizes))
    parts = [left_of(k, high) for k in early]
    held = [add(part, inward(part)) for part in parts]
    high, held[0] = together(high, held[0])
    part = left_of(final, high)
    held.append(add(part, inward(part)))
    crossed = [add(x, across(x)) for x in held[:-1]]
    held[-1], crossed[0] = together(held[-1], crossed[0])
    crossed.append(add(held[-1], across(held[-1])))
    lefts = [choose(order, x, outward(x)) for x in crossed]

    groups = ((7, 6), (3, 2), (5, 4), (1, 0))
    sums = []
    for k in early:
        sums = raw_pieces(order, groups, lefts[k], resident, starts[k], sums, 1)
    *sums, gram = sums

    def last(order, g):
        return raw_pieces(order, groups[g : g + 1], lefts[-1], resident, starts[-1], [sums[g]], 0)[0]

    sent_far = last(order, 0)
    order_1, sent_far = together(order, sent_far)
    halves = gram_halves(order_1, lefts[-1], gram)
    order_2, halves = together(order_1, halves)
    kept_far = last(order_2, 1)
    kept_far = add(kept_far, along(sent_far, PAIR))
    got_near = along(kept_far, NEAR)
    kept = add(halves[0], along(halves[1], PAIR))
    order_3, kept_far, kept = together(order_2, kept_far, kept)
    sent_near, kept_near = last(order_3, 2), last(order_3, 3)
    kept = add(kept, *[along(kept, pairs) for pairs in (NEAR, FAR, ACROSS)])
    got_near, kept = together(got_near, kept)
    slot_0, slot_1 = add_halves(kept_near, along(sent_near, PAIR), got_near)
    got_own = along(slot_1, FAR)
    inverse, orth, operand = factor(order, kept, along(kept, PAIR), lefts)
    got_own, inverse = together(got_own, inverse)
    own = add(slot_0, got_own)

    def new_pair(slot, raws, before):
        return new_chunks(order, (slot, slot + 4), operand, inverse, raws, resident, before)

    chunk_1, pair = along(own, FAR), along(own, PAIR)
    squares = square_row(inverse, own)
    squares = add(squares, along(squares, PAIR))
    squares, again = together(squares, own)
    got, chunk_2 = along(squares, NEAR), along(again, NEAR)
    new, rights = new_chunks(order, (0, 4), operand, inverse, [own, pair], resident, [])
    got, chunk_1, new[0] = together(got, chunk_1, new[0])
    chunk_3, pair_1 = along(chunk_1, NEAR), along(chunk_1, PAIR)
    squares = add(squares, got)
    gots = [lax.ppermute(squares, "col", [(c, c ^ d) for c in range(LINE)]) for d in range(1, LINE)]
    pair_1, chunk_2 = together(pair_1, chunk_2)
    new, right = new_chunks(order, (1, 5), operand, inverse, [chunk_1, pair_1], resident, new)
    rights += right
    *gots, chunk_2, chunk_3, new[0] = together(*gots, chunk_2, chunk_3, new[0])
    pair_2, pair_3 = along(chunk_2, PAIR), along(chunk_3, PAIR)
    squares = add(squares, *gots)
    scaled = update_operand([squares, along(squares, FAR)], orth, scale)
    raws = [chunk_2, pair_2, chunk_3, pair_3]
    return tuple(
        finish(order, (2, 6, 3, 7), (0, 4, 1, 5), operand, scaled, inverse, resident, raws, rights, new[0])
    )


def general(momentum, right_factor, scale):
    left = lax.psum(jnp.dot(momentum, right_factor, precision=HIGHEST), "col")
    gram_part = jnp.dot(left.T, left, precision=HIGHEST)
    raw_part = jnp.dot(left.T, momentum, precision=HIGHEST)
    gram, raw = lax.psum((gram_part, raw_part), "row")
    lower = jnp.linalg.cholesky(gram)
    orth = jax.scipy.linalg.solve_triangular(lower, left.T, lower=True).T
    right = jax.scipy.linalg.solve_triangular(lower, raw, lower=True)
    squares = lax.psum(jnp.sum(right * right, axis=1, keepdims=True), "col")
    factor_q = right / jnp.sqrt(squares + 1e-06)
    new = momentum - 0.5 * jnp.dot(orth, right, precision=HIGHEST)
    return new, scale * jnp.dot(orth, factor_q, precision=HIGHEST)


def solution(mesh):
    by_hand = mesh.shape["row"] == RING and mesh.shape["col"] == LINE
    program = local if by_hand else general

    def run(momentum, right_factor):
        rows, cols = momentum.shape
        scale = math.sqrt(rows * cols / right_factor.shape[1])
        return jax.shard_map(
            lambda m, q: program(m, q, scale),
            mesh=mesh,
            in_specs=(P("row", "col"), P("col", None)),
            out_specs=(P("row", "col"), P("row", "col")),
            check_vma=False,
        )(momentum, right_factor)

    return run
```
